256 devices in a mesh: tok: 16 (over z, x_lo), head: 16 (over x_hi, y, core).
Axes of the slice: x: 4 (x_hi: 2, x_lo: 2; x = x_hi * 2 + x_lo), y: 4, z: 8, core: 2. Of those that a mesh axis runs over, the one named last changes fastest.
Arguments:
- tri_tokens: bfloat16 [8192, 1024], P(('tok', 'head')), may hold values from -6 to 6
- image_tokens: bfloat16 [65536, 1024], P('tok'), may hold values from -6 to 6
- cross_q: bfloat16 [1024, 1024], P(None, 'head'), may hold values from -0.1875 to 0.1875
- cross_kv: bfloat16 [2, 1024, 1024], P(None, None, 'head'), may hold values from -0.1875 to 0.1875
- cross_out: bfloat16 [1024, 1024], P('head'), may hold values from -0.1875 to 0.1875
- self_qkv: bfloat16 [3, 1024, 1024], P(None, None, 'head'), may hold values from -0.1875 to 0.1875
- self_out: bfloat16 [1024, 1024], P('head'), may hold values from -0.1875 to 0.1875
- mlp_in: bfloat16 [1024, 4096], P(None, 'head'), may hold values from -0.1875 to 0.1875
- mlp_out: bfloat16 [4096, 1024], P('head'), may hold values from -0.09375 to 0.09375
Outputs:
- tri_out: bfloat16 [8192, 1024], P(('tok', 'head'))
The draws below stay inside these ranges and needn't reach their ends.
All inputs are finite; a program needn't handle non-finite values.
Results may differ from the reference program's by a relative error of at most 0.013.
Values may be sent and summed in bfloat16 or wider, within the bound.
No kernel may reach another device: no remote copies, remote signals or barrier semaphores. Data moves between devices by JAX's collectives and lax.ppermute only.
A program may use at most 128 MiB of HBM per device.

```python
import math
import jax
import jax.numpy as jnp
from jax import lax

D = 1024
HEADS = 16
FF = 4096
TRI = 8192
IMG = 65536


def level_of(key, extent, cuts, least, top_value):
    factor_of = 1.0
    for axis_at, blocks in cuts:
        steps = jax.random.uniform(jax.random.fold_in(jax.random.fold_in(key, 6), axis_at), (blocks,), jnp.float32, least / len(cuts), top_value / len(cuts))
        factor_of = factor_of * jnp.repeat(jnp.exp(steps), extent[axis_at] // blocks).reshape((-1,) + (1,) * (len(extent) - 1 - axis_at))
    return factor_of


def scatter_about(rng, extent, deviation, reach, pieces=(), dtype=jnp.bfloat16):
    values = jax.random.normal(rng, extent, jnp.float32) * deviation
    if len(pieces) > 0:
        values = level_of(rng, extent, pieces, -0.22, 0.18) * values
    return jnp.clip(values, min=-reach, max=reach).astype(dtype)


def setup_inputs(seed: int = 0) -> dict:
    key_of = jax.random.split(jax.random.key(seed), 10)
    return {
        "tri_tokens": scatter_about(key_of[0], (TRI, D), 1.0, 6.0, ((0, 256),)),
        "image_tokens": scatter_about(key_of[1], (IMG, D), 1.0, 6.0, ((0, 16),)),
        "cross_q": scatter_about(key_of[2], (D, D), D ** -0.5, 0.1875, ((1, 16),)),
        "cross_kv": scatter_about(key_of[3], (2, D, D), D ** -0.5, 0.1875, ((2, 16),)),
        "cross_out": scatter_about(key_of[4], (D, D), D ** -0.5, 0.1875, ((0, 16),)),
        "self_qkv": scatter_about(key_of[5], (3, D, D), D ** -0.5, 0.1875, ((2, 16),)),
        "self_out": scatter_about(key_of[6], (D, D), D ** -0.5, 0.1875, ((0, 16),)),
        "mlp_in": scatter_about(key_of[7], (D, FF), D ** -0.5, 0.1875, ((1, 16),)),
        "mlp_out": scatter_about(key_of[8], (FF, D), FF ** -0.5, 0.09375, ((0, 16),)),
    }


score_gain = 2.5

def layer_norm(values):
    centered = values - lax.optimization_barrier(jnp.mean(values, axis=-1, keepdims=True))
    return centered * lax.rsqrt(lax.optimization_barrier(jnp.mean(centered * centered, axis=-1, keepdims=True)) + 1e-05)

def head_norm(values, head_count):
    shaped = values.reshape(values.shape[0], head_count, -1)
    normed = shaped * lax.rsqrt(lax.optimization_barrier(jnp.mean(shaped * shaped, axis=-1, keepdims=True)) + 1e-06)
    return normed.reshape(values.shape[0], -1).astype(jnp.bfloat16)

def partial_attention(queries, kv_rows, head_count):
    query_count = queries.shape[0]
    head_size = queries.shape[1] // head_count
    score_scale = score_gain / math.sqrt(head_size)
    query_block = math.gcd(query_count, 512)
    key_block = math.gcd(kv_rows.shape[0], 2048)
    query_blocks = queries.reshape(query_count // query_block, query_block, head_count, head_size)
    key_blocks = kv_rows.reshape(kv_rows.shape[0] // key_block, key_block, 2, head_count, head_size)

    def one_block(query_tile):

        def key_step(running, key_tile):
            weighted, totals = running
            scores = jnp.einsum('qhd,khd->qhk', query_tile, key_tile[:, 0], preferred_element_type=jnp.float32) * score_scale
            exp_scores = jnp.exp(scores)
            totals = totals + lax.optimization_barrier(jnp.sum(exp_scores, axis=-1))
            weighted = weighted + jnp.einsum('qhk,khd->qhd', exp_scores.astype(jnp.bfloat16), key_tile[:, 1], preferred_element_type=jnp.float32)
            return ((weighted, totals), None)
        starting = (jnp.zeros((query_block, head_count, head_size), jnp.float32), jnp.zeros((query_block, head_count), jnp.float32))
        result, _ = lax.scan(key_step, starting, key_blocks)
        return result
    weighted, totals = lax.map(one_block, query_blocks)
    return (weighted.reshape(query_count, head_count, head_size), totals.reshape(query_count, head_count))

def finish(weighted, totals):
    return (weighted / totals[:, :, None]).reshape(weighted.shape[0], -1).astype(jnp.bfloat16)

def reference(tri_tokens, image_tokens, cross_q, cross_kv, cross_out, self_qkv, self_out, mlp_in, mlp_out):
    stream_zero = tri_tokens.astype(jnp.float32)
    normed_one = layer_norm(stream_zero).astype(jnp.bfloat16)
    queries = head_norm(jnp.dot(normed_one, cross_q, preferred_element_type=jnp.float32), HEADS)
    kv_weight = jnp.concatenate([cross_kv[0], cross_kv[1]], axis=1)
    image_kv = jnp.dot(image_tokens, kv_weight, preferred_element_type=jnp.float32)
    view_kv = jnp.concatenate([head_norm(image_kv[:, :D], HEADS), image_kv[:, D:].astype(jnp.bfloat16)], axis=1)
    weighted, totals = partial_attention(queries, view_kv, HEADS)
    cross_mix = finish(weighted, totals)
    stream_one = stream_zero + jnp.dot(cross_mix, cross_out, preferred_element_type=jnp.float32)
    normed_two = layer_norm(stream_one).astype(jnp.bfloat16)
    self_weight = jnp.concatenate([self_qkv[0], self_qkv[1], self_qkv[2]], axis=1)
    mixed = jnp.dot(normed_two, self_weight, preferred_element_type=jnp.float32)
    self_queries = head_norm(mixed[:, :D], HEADS)
    self_kv = jnp.concatenate([head_norm(mixed[:, D:2 * D], HEADS), mixed[:, 2 * D:].astype(jnp.bfloat16)], axis=1)
    weighted, totals = partial_attention(self_queries, self_kv, HEADS)
    self_mix = finish(weighted, totals)
    stream_two = stream_one + jnp.dot(self_mix, self_out, preferred_element_type=jnp.float32)
    normed_three = layer_norm(stream_two).astype(jnp.bfloat16)
    hidden = jax.nn.gelu(jnp.dot(normed_three, mlp_in, preferred_element_type=jnp.float32), approximate=True).astype(jnp.bfloat16)
    return (stream_two + jnp.dot(hidden, mlp_out, preferred_element_type=jnp.float32)).astype(jnp.bfloat16)
```

```python
import functools
import math

import jax
import jax.numpy as jnp
from jax import lax
from jax.experimental import pallas as pl
from jax.experimental.pallas import tpu as pltpu
from jax.sharding import Mesh, PartitionSpec as P

HEAD_SIZE = 64
EXT = 80
SCORE = 2.5 / math.sqrt(HEAD_SIZE) * math.log2(math.e)
PLANE = ("xh", "y")
HEAD = ("xh", "y", "c")


def layer_norm(values):
    centered = values - jnp.mean(values, axis=-1, keepdims=True)
    return centered * lax.rsqrt(jnp.mean(centered * centered, axis=-1, keepdims=True) + 1e-05)


def column_norm(values):
    return values * lax.rsqrt(jnp.mean(values * values, axis=0, keepdims=True) + 1e-06)


def project_kv_kernel(image_ref, weight_ref, out_ref):
    product = jnp.dot(image_ref[...], weight_ref[...], preferred_element_type=jnp.float32).T
    out_ref[:HEAD_SIZE] = column_norm(product[:HEAD_SIZE]).astype(jnp.bfloat16)
    out_ref[HEAD_SIZE:] = product[HEAD_SIZE:].astype(jnp.bfloat16)


def project_kv(image_tokens, weight):
    rows, features = image_tokens.shape
    block = 512
    return pl.pallas_call(
        project_kv_kernel,
        grid=(rows // block,),
        in_specs=[
            pl.BlockSpec((block, features), lambda i: (i, 0)),
            pl.BlockSpec(weight.shape, lambda i: (0, 0)),
        ],
        out_specs=pl.BlockSpec((2 * HEAD_SIZE, block), lambda i: (0, i)),
        out_shape=jax.ShapeDtypeStruct((2 * HEAD_SIZE, rows), jnp.bfloat16),
        compiler_params=pltpu.CompilerParams(vmem_limit_bytes=32 * 2**20),
        name="project_kv",
    )(image_tokens, weight)


def attention_kernel(step, piece_count, query_ref, *refs):
    pieces = refs[:piece_count]
    out_ref, keys, values = refs[piece_count:]
    width = pieces[0].shape[-1]

    @pl.when(pl.program_id(0) == 0)
    def _():
        first = 0
        for piece in pieces:
            for i in range(piece.shape[0]):
                keys[first : first + width, :] = piece[i, :HEAD_SIZE].T
                values[:HEAD_SIZE, first : first + width] = piece[i, HEAD_SIZE:]
                first += width
        row = lax.broadcasted_iota(jnp.int32, (EXT - HEAD_SIZE, values.shape[1]), 0)
        values[HEAD_SIZE:] = jnp.where(row == 0, 1.0, 0.0).astype(jnp.bfloat16)

    queries = query_ref[...]
    total = jnp.zeros((EXT, queries.shape[1]), jnp.float32)
    for first in range(0, keys.shape[0], step):
        scores = jnp.dot(
            keys[first : first + step, :], queries, preferred_element_type=jnp.float32
        )
        weights = jnp.exp2(scores).astype(jnp.bfloat16)
        total = total + jnp.dot(
            values[:, first : first + step], weights, preferred_element_type=jnp.float32
        )
    out_ref[...] = total.astype(out_ref.dtype)


def attention(queries, pieces, step=1024):
    blocks, _, width = queries.shape
    key_count = sum(piece.shape[0] * piece.shape[2] for piece in pieces)
    return pl.pallas_call(
        functools.partial(attention_kernel, step, len(pieces)),
        grid=(blocks,),
        in_specs=[pl.BlockSpec((None, HEAD_SIZE, width), lambda i: (i, 0, 0))]
        + [pl.BlockSpec(piece.shape, lambda i: (0, 0, 0)) for piece in pieces],
        out_specs=pl.BlockSpec((None, EXT, width), lambda i: (i, 0, 0)),
        out_shape=jax.ShapeDtypeStruct((blocks, EXT, width), jnp.bfloat16),
        scratch_shapes=[
            pltpu.VMEM((key_count, HEAD_SIZE), jnp.bfloat16),
            pltpu.VMEM((EXT, key_count), jnp.bfloat16),
        ],
        compiler_params=pltpu.CompilerParams(vmem_limit_bytes=48 * 2**20),
        name="attention",
    )(queries, *pieces)


def exchange(values, axes):
    return lax.all_to_all(values, axes, 0, 0, tiled=True)


def share(values, axes, count):
    return exchange(jnp.broadcast_to(values, (count,) + values.shape), axes)


def share_head(values, plane):
    return lax.all_gather(share(values, PLANE, plane), "c", axis=1)


def finish(partials):
    total = jnp.sum(partials.astype(jnp.float32), axis=0)
    return (total[:HEAD_SIZE] / total[HEAD_SIZE : HEAD_SIZE + 1]).astype(jnp.bfloat16)


def across(left, right, dims):
    return lax.dot_general(left, right, (dims, ((), ())), preferred_element_type=jnp.float32)


def per_device(
    sizes,
    tri_tokens,
    image_tokens,
    cross_q,
    cross_kv,
    cross_out,
    self_qkv,
    self_out,
    mlp_in,
    mlp_out,
):
    width = tri_tokens.shape[1]
    plane = sizes["xh"] * sizes["y"]
    rows = tri_tokens.shape[0] * plane * sizes["c"]

    cross_out_all = lax.all_gather(cross_out, HEAD, axis=0, tiled=True)
    self_out_all = lax.all_gather(self_out, HEAD, axis=0, tiled=True)

    tri_group = share_head(tri_tokens, plane).reshape(rows, width)
    image_kv = project_kv(image_tokens, jnp.concatenate([cross_kv[0], cross_kv[1]], axis=1))
    other_kv = lax.ppermute(image_kv, "xl", [(0, 1), (1, 0)])
    stream_zero = tri_group.astype(jnp.float32)
    normed = layer_norm(stream_zero).astype(jnp.bfloat16)
    queries = (column_norm(across(cross_q, normed, ((0,), (1,)))) * SCORE).astype(jnp.bfloat16)
    z_axes = ("za", "zb")
    z_count = sizes["za"] * sizes["zb"]
    all_queries = share(queries, z_axes, z_count)
    partials = attention(all_queries, [image_kv[None], other_kv[None]])
    mix = finish(exchange(partials, z_axes))
    mix_all = share_head(mix, plane).reshape(width, rows)
    stream_one = stream_zero + across(mix_all, cross_out_all, ((0,), (0,)))

    normed = layer_norm(stream_one).astype(jnp.bfloat16)
    self_weight = jnp.concatenate([self_qkv[0], self_qkv[1], self_qkv[2]], axis=1)
    mixed = across(self_weight, normed, ((0,), (1,)))
    queries = (column_norm(mixed[:HEAD_SIZE]) * SCORE).astype(jnp.bfloat16)
    self_kv = jnp.concatenate(
        [
            column_norm(mixed[HEAD_SIZE : 2 * HEAD_SIZE]).astype(jnp.bfloat16),
            mixed[2 * HEAD_SIZE :].astype(jnp.bfloat16),
        ],
        axis=0,
    )
    pair = ("zb", "xl")
    all_kv = share(self_kv, "za", sizes["za"])
    all_queries = share(queries, pair, sizes["zb"] * sizes["xl"])
    partials = attention(all_queries, [all_kv])
    mix = finish(exchange(partials, pair))
    mix_all = share_head(mix, plane).reshape(width, rows)
    stream_two = stream_one + across(mix_all, self_out_all, ((0,), (0,)))

    normed = layer_norm(stream_two).astype(jnp.bfloat16)
    hidden = jax.nn.gelu(
        jnp.dot(normed, mlp_in, preferred_element_type=jnp.float32), approximate=True
    ).astype(jnp.bfloat16)
    product = jnp.dot(hidden, mlp_out, preferred_element_type=jnp.float32)
    product = product.astype(jnp.bfloat16).reshape(plane, sizes["c"], -1, width)
    core = lax.axis_index("c")
    kept = lax.dynamic_index_in_dim(product, core, 1, keepdims=False)
    given = lax.dynamic_index_in_dim(product, 1 - core, 1, keepdims=False)
    got = lax.ppermute(given, "c", [(0, 1), (1, 0)])
    both = (kept.astype(jnp.float32) + got.astype(jnp.float32)).astype(jnp.bfloat16)
    collected = jnp.sum(exchange(both, PLANE).astype(jnp.float32), axis=0)
    place = lax.axis_index(HEAD) * tri_tokens.shape[0]
    own = lax.dynamic_slice_in_dim(stream_two, place, tri_tokens.shape[0], axis=0)
    return (own + collected).astype(jnp.bfloat16)


def solution(mesh):
    sizes = {"za": 4, "zb": 2, "xl": 2, "xh": 2, "y": 4, "c": 2}
    names = tuple(sizes)
    fine = Mesh(mesh.devices.reshape(tuple(sizes.values())), names)
    tok = ("za", "zb", "xl")
    return jax.shard_map(
        functools.partial(per_device, sizes),
        mesh=fine,
        in_specs=(
            P(names, None),
            P(tok, None),
            P(None, HEAD),
            P(None, None, HEAD),
            P(HEAD, None),
            P(None, None, HEAD),
            P(HEAD, None),
            P(None, HEAD),
            P(HEAD, None),
        ),
        out_specs=P(names, None),
        check_vma=False,
    )
```

```python
import functools
import math

import jax
import jax.numpy as jnp
from jax import lax
from jax.experimental import pallas as pl
from jax.experimental.pallas import tpu as pltpu
from jax.sharding import Mesh, PartitionSpec as P

HEAD_SIZE = 64
EXT = 80
VMEM_LIMIT = 20 * 2**20
SCORE = 2.5 / math.sqrt(HEAD_SIZE) * math.log2(math.e)
PLANE = ("xh", "y")
HEAD = ("xh", "y", "c")


def layer_norm(values):
    centered = values - jnp.mean(values, axis=-1, keepdims=True)
    return centered * lax.rsqrt(jnp.mean(centered * centered, axis=-1, keepdims=True) + 1e-05)


def column_norm(values):
    return values * lax.rsqrt(jnp.mean(values * values, axis=0, keepdims=True) + 1e-06)


def kernel_call(body, out_shape, name, flops, scratch=(), scalars=0, count=0):
    scalar = [pl.BlockSpec(memory_space=pltpu.SMEM)] * scalars
    return pl.pallas_call(
        body,
        in_specs=scalar + [pl.BlockSpec(memory_space=pltpu.VMEM)] * count,
        out_specs=jax.tree.map(lambda _: pl.BlockSpec(memory_space=pltpu.VMEM), out_shape),
        out_shape=out_shape,
        scratch_shapes=scratch,
        compiler_params=pltpu.CompilerParams(vmem_limit_bytes=VMEM_LIMIT),
        cost_estimate=pl.CostEstimate(flops=flops, transcendentals=0, bytes_accessed=2**20),
        name=name,
    )


def bf16(*shape):
    return jax.ShapeDtypeStruct(shape, jnp.bfloat16)


def ones_rows(count):
    row = lax.broadcasted_iota(jnp.int32, (EXT - HEAD_SIZE, count), 0)
    return jnp.where(row == 0, 1.0, 0.0).astype(jnp.bfloat16)


def project_kv_kernel(image_ref, weight_ref, both_ref, key_ref, value_ref):
    product = jnp.dot(image_ref[...], weight_ref[...], preferred_element_type=jnp.float32).T
    keys = column_norm(product[:HEAD_SIZE]).astype(jnp.bfloat16)
    values = product[HEAD_SIZE:].astype(jnp.bfloat16)
    both_ref[:HEAD_SIZE] = keys
    both_ref[HEAD_SIZE:] = values
    key_ref[...] = keys.T
    value_ref[:HEAD_SIZE] = values
    value_ref[HEAD_SIZE:] = ones_rows(values.shape[1])


def project_kv(image_tokens, weight):
    rows, features = image_tokens.shape
    block = 512
    return pl.pallas_call(
        project_kv_kernel,
        grid=(rows // block,),
        in_specs=[
            pl.BlockSpec((block, features), lambda i: (i, 0)),
            pl.BlockSpec(weight.shape, lambda i: (0, 0)),
        ],
        out_specs=[
            pl.BlockSpec((2 * HEAD_SIZE, block), lambda i: (0, i)),
            pl.BlockSpec((block, HEAD_SIZE), lambda i: (i, 0)),
            pl.BlockSpec((EXT, block), lambda i: (0, i)),
        ],
        out_shape=[bf16(2 * HEAD_SIZE, rows), bf16(rows, HEAD_SIZE), bf16(EXT, rows)],
        compiler_params=pltpu.CompilerParams(vmem_limit_bytes=VMEM_LIMIT),
        cost_estimate=pl.CostEstimate(
            flops=6 * 10**9, transcendentals=0, bytes_accessed=rows * features * 2
        ),
        name="project_kv",
    )(image_tokens, weight)


def prepare_kernel(both_ref, key_ref, value_ref):
    key_ref[...] = both_ref[:HEAD_SIZE].T
    value_ref[:HEAD_SIZE] = both_ref[HEAD_SIZE:]
    value_ref[HEAD_SIZE:] = ones_rows(both_ref.shape[1])


def prepare(both):
    rows = both.shape[1]
    return kernel_call(
        prepare_kernel, [bf16(rows, HEAD_SIZE), bf16(EXT, rows)], "prepare", 10**9, count=1
    )(both)


def attend(queries, pieces, step):
    total = jnp.zeros((EXT, queries.shape[1]), jnp.float32)
    for keys, values in pieces:
        for first in range(0, keys.shape[0], step):
            scores = jnp.dot(
                keys[first : first + step, :], queries, preferred_element_type=jnp.float32
            )
            weights = jnp.exp2(scores).astype(jnp.bfloat16)
            total = total + jnp.dot(
                values[:, first : first + step], weights, preferred_element_type=jnp.float32
            )
    return total


def cross_kernel(query_count, carried, step, *refs):
    queries = [ref[...] for ref in refs[:query_count]]
    keys, values, *rest = refs[query_count:]
    together = queries[0] if query_count == 1 else jnp.concatenate(queries, axis=1)
    total = attend(together, [(keys, values)], step)
    width = queries[0].shape[1]
    outs = rest[query_count:] if carried else rest
    for i, out in enumerate(outs):
        part = total[:, i * width : (i + 1) * width]
        if carried:
            part = part + rest[i][...]
        out[...] = part.astype(out.dtype)


def cross_attention(queries, piece, carried=None):
    width = queries[0].shape[1]
    count = len(queries)
    kind = jnp.float32 if carried is None else jnp.bfloat16
    extra = [] if carried is None else carried
    return kernel_call(
        functools.partial(cross_kernel, count, carried is not None, 1024 if count == 1 else 512),
        [jax.ShapeDtypeStruct((EXT, width), kind)] * count,
        "cross_attention",
        16 * HEAD_SIZE * width * count * piece[0].shape[0],
        count=count + 2 + len(extra),
    )(*queries, *piece, *extra)


def self_kernel(query_count, piece_count, carried, *refs):
    queries = jnp.concatenate([ref[...] for ref in refs[:query_count]], axis=1)
    pieces = refs[query_count : query_count + piece_count]
    rest = refs[query_count + piece_count :]
    outs = rest[query_count:] if carried else rest
    width = pieces[0].shape[1]
    total = jnp.zeros((EXT, queries.shape[1]), jnp.float32)
    for piece in pieces:
        values = jnp.concatenate([piece[HEAD_SIZE:], ones_rows(width)], axis=0)
        total = total + attend(queries, [(piece[:HEAD_SIZE].T, values)], width)
    for i, out in enumerate(outs):
        part = total[:, i * width : (i + 1) * width]
        if carried:
            part = part + rest[i][...]
        out[...] = part.astype(out.dtype)


def self_attention(queries, pieces, carried=None, kind=jnp.float32):
    width = queries[0].shape[1]
    count = len(queries)
    extra = [] if carried is None else carried
    return kernel_call(
        functools.partial(self_kernel, count, len(pieces), carried is not None),
        [jax.ShapeDtypeStruct((EXT, width), kind)] * count,
        "self_attention",
        16 * HEAD_SIZE * width * count * width * len(pieces),
        count=count + len(pieces) + len(extra),
    )(*queries, *pieces, *extra)


def finish_kernel(*refs):
    out_ref = refs[-1]
    parts = []
    for ref in refs[:-1]:
        parts += [ref[i] for i in range(ref.shape[0])] if len(ref.shape) == 3 else [ref[...]]
    total = functools.reduce(lambda x, y: x + y, [part.astype(jnp.float32) for part in parts])
    mix = (total[:HEAD_SIZE] / total[HEAD_SIZE : HEAD_SIZE + 1]).astype(jnp.bfloat16)
    for i in range(out_ref.shape[0]):
        out_ref[i] = mix


def finish(partials, copies):
    width = partials[0].shape[-1]
    return kernel_call(
        finish_kernel, bf16(copies, HEAD_SIZE, width), "finish", 10**8, count=len(partials)
    )(*partials)


def place_rows(target, core, mine, other):
    plane, size, _ = mine.shape
    for i in range(plane):
        first = pl.multiple_of((2 * i + core) * size, size)
        target[pl.ds(first, size), :] = mine[i]
        first = pl.multiple_of((2 * i + 1 - core) * size, size)
        target[pl.ds(first, size), :] = other[i]


def first_kernel(core_ref, mine_ref, other_ref, weight_ref, query_ref, rows):
    place_rows(rows, core_ref[0], mine_ref, other_ref)
    normed = layer_norm(rows[...].astype(jnp.float32)).astype(jnp.bfloat16)
    product = jnp.dot(normed, weight_ref[...], preferred_element_type=jnp.float32).T
    query_ref[...] = (column_norm(product) * SCORE).astype(jnp.bfloat16)


def first_stage(core, mine, other, weight):
    plane, size, width = mine.shape
    rows = 2 * plane * size
    return kernel_call(
        first_kernel,
        bf16(HEAD_SIZE, rows),
        "first_stage",
        10**9,
        [pltpu.VMEM((rows, width), jnp.bfloat16)],
        scalars=1,
        count=3,
    )(core, mine, other, weight)


def middle_kernel(
    core_ref, mine_ref, other_ref, out_w, tri_mine, tri_other, qkv_w,
    stream_ref, query_ref, kv_ref, mix, rows,
):
    core = core_ref[0]
    place_rows(mix, core, mine_ref, other_ref)
    place_rows(rows, core, tri_mine, tri_other)
    stream = rows[...].astype(jnp.float32) + jnp.dot(
        mix[...].T, out_w[...], preferred_element_type=jnp.float32
    )
    stream_ref[...] = stream
    normed = layer_norm(stream).astype(jnp.bfloat16)
    product = jnp.dot(normed, qkv_w[...], preferred_element_type=jnp.float32).T
    query_ref[...] = (column_norm(product[:HEAD_SIZE]) * SCORE).astype(jnp.bfloat16)
    kv_ref[:HEAD_SIZE] = column_norm(product[HEAD_SIZE : 2 * HEAD_SIZE]).astype(jnp.bfloat16)
    kv_ref[HEAD_SIZE:] = product[2 * HEAD_SIZE :].astype(jnp.bfloat16)


def middle_stage(core, mine, other, out_w, tri_parts, qkv_w):
    plane, size, width = tri_parts[0].shape
    count = 2 * plane * size
    return kernel_call(
        middle_kernel,
        [
            jax.ShapeDtypeStruct((count, width), jnp.float32),
            bf16(HEAD_SIZE, count),
            bf16(2 * HEAD_SIZE, count),
        ],
        "middle_stage",
        3 * 10**9,
        [pltpu.VMEM((width, count), jnp.bfloat16), pltpu.VMEM((count, width), jnp.bfloat16)],
        scalars=1,
        count=6,
    )(core, mine, other, out_w, *tri_parts, qkv_w)


def last_kernel(
    core_ref, mine_ref, other_ref, out_w, stream_ref, in_w, down_w,
    own_ref, kept_ref, given_ref, mix, rows,
):
    core = core_ref[0]
    place_rows(mix, core, mine_ref, other_ref)
    stream = stream_ref[...] + jnp.dot(
        mix[...].T, out_w[...], preferred_element_type=jnp.float32
    )
    rows[...] = stream
    plane, size, _ = kept_ref.shape
    own_ref[...] = rows[pl.ds(pl.multiple_of(core_ref[1] * size, size), size), :]
    normed = layer_norm(stream).astype(jnp.bfloat16)
    hidden = jax.nn.gelu(
        jnp.dot(normed, in_w[...], preferred_element_type=jnp.float32), approximate=True
    ).astype(jnp.bfloat16)
    rows[...] = jnp.dot(hidden, down_w[...], preferred_element_type=jnp.float32)
    for i in range(plane):
        first = pl.multiple_of((2 * i + core) * size, size)
        kept_ref[i] = rows[pl.ds(first, size), :].astype(jnp.bfloat16)
        first = pl.multiple_of((2 * i + 1 - core) * size, size)
        given_ref[i] = rows[pl.ds(first, size), :].astype(jnp.bfloat16)


def last_stage(core, mine, other, out_w, stream, in_w, down_w, size):
    count, width = stream.shape
    plane = mine.shape[0]
    return kernel_call(
        last_kernel,
        [
            jax.ShapeDtypeStruct((size, width), jnp.float32),
            bf16(plane, size, width),
            bf16(plane, size, width),
        ],
        "last_stage",
        4 * 10**9,
        [pltpu.VMEM((width, count), jnp.bfloat16), pltpu.VMEM((count, width), jnp.float32)],
        scalars=1,
        count=6,
    )(core, mine, other, out_w, stream, in_w, down_w)


def exchange(values, axes):
    return lax.all_to_all(values, axes, 0, 0, tiled=True)


def copies_of(values, count):
    return jnp.broadcast_to(values, (count,) + values.shape)


def other_core(values):
    return lax.ppermute(values, "c", [(0, 1), (1, 0)])


def swap_near(values):
    return lax.ppermute(values, "xl", [(0, 1), (1, 0)])


def gather_head(copies):
    mine = exchange(copies, PLANE)
    return mine, other_core(mine)


def per_device(
    sizes,
    tri_tokens,
    image_tokens,
    cross_q,
    cross_kv,
    cross_out,
    self_qkv,
    self_out,
    mlp_in,
    mlp_out,
):
    size, width = tri_tokens.shape
    plane = sizes["xh"] * sizes["y"]
    z_axes = ("zh", "zl")
    z_count = sizes["zh"] * sizes["zl"]

    def along(values, shift):
        return lax.ppermute(values, z_axes, [(i, (i + shift) % z_count) for i in range(z_count)])

    core = jnp.stack([lax.axis_index("c"), lax.axis_index(HEAD)]).astype(jnp.int32)
    cross_out_all = lax.all_gather(cross_out, HEAD, axis=0, tiled=True)
    self_out_all = lax.all_gather(self_out, HEAD, axis=0, tiled=True)

    mine = exchange(copies_of(tri_tokens, plane), PLANE)
    both, keys, values = project_kv(
        image_tokens, jnp.concatenate([cross_kv[0], cross_kv[1]], axis=1)
    )
    mine, both = lax.optimization_barrier((mine, both))
    other = other_core(mine)
    near = (keys, values)
    tri_parts = (mine, other)
    own = first_stage(core, mine, other, cross_q)

    def behind(value, done):
        return value if done is None else lax.optimization_barrier((value, done))[0]

    arrived = {0: own}
    sums = {None: None}

    def relay(block, shift, done):
        arrived[block - shift] = along(behind(arrived[block], sums[done]), shift)

    def near_part(block, done):
        (sums[block],) = cross_attention([behind(arrived[block], sums[done])], near)

    relay(0, 1, None)
    near_part(0, None)
    relay(0, -1, 0)
    relay(-1, 1, 0)
    near_part(-1, 0)
    relay(1, -1, -1)
    near_part(1, -1)
    relay(-2, 1, 1)
    near_part(-2, 1)
    relay(2, -1, -2)
    near_part(2, -2)
    relay(-3, 1, 2)
    near_part(-3, 2)
    near_part(3, -3)
    near_part(-4, 3)
    swapped = swap_near(both)
    far = prepare(behind(swapped, sums[3]))
    returned = []
    last = None
    for place, block in enumerate((-4, -3, 3, -2, 2, -1, 1, 0)):
        query = behind(arrived[block], last)
        if block == -1:
            query, cross_out_all = lax.optimization_barrier((query, cross_out_all))
        if place >= 6:
            query, returned[place - 6] = lax.optimization_barrier((query, returned[place - 6]))
        (last,) = cross_attention([query], far, [sums[block]])
        returned.append(along(last, block) if block else last)
    partials = returned
    mine, other = gather_head(finish(partials, plane))
    self_weight = jnp.concatenate([self_qkv[0], self_qkv[1], self_qkv[2]], axis=1)
    stream, own, own_kv = middle_stage(
        core, mine, other, cross_out_all, tri_parts, self_weight
    )

    own, self_out_all = lax.optimization_barrier((own, self_out_all))
    left, right = along(own_kv, 1), along(own_kv, -1)
    queries = [own, swap_near(own)]
    carried = self_attention(queries, [own_kv])
    for step in range(3):
        blocks = [left, right]
        held, carried = lax.optimization_barrier((blocks, carried))
        left = along(held[0], 1)
        if step < 2:
            right = along(held[1], -1)
        carried = self_attention(queries, blocks, carried)
    here, there = self_attention(queries, [left], carried, jnp.bfloat16)
    mine, other = gather_head(finish([here, swap_near(there)], plane))
    own, kept, given = last_stage(
        core, mine, other, self_out_all, stream, mlp_in, mlp_out, size
    )
    got = other_core(given)
    both = (kept.astype(jnp.float32) + got.astype(jnp.float32)).astype(jnp.bfloat16)
    collected = jnp.sum(exchange(both, PLANE).astype(jnp.float32), axis=0)
    return (own + collected).astype(jnp.bfloat16)


def solution(mesh):
    sizes = {"zh": 2, "zl": 4, "xl": 2, "xh": 2, "y": 4, "c": 2}
    names = tuple(sizes)
    fine = Mesh(mesh.devices.reshape(tuple(sizes.values())), names)
    tok = ("zh", "zl", "xl")
    return jax.shard_map(
        functools.partial(per_device, sizes),
        mesh=fine,
        in_specs=(
            P(names, None),
            P(tok, None),
            P(None, HEAD),
            P(None, None, HEAD),
            P(HEAD, None),
            P(None, None, HEAD),
            P(HEAD, None),
            P(None, HEAD),
            P(HEAD, None),
        ),
        out_specs=P(names, None),
        check_vma=False,
    )
```

```python
import functools
import math

import jax
import jax.numpy as jnp
from jax import lax
from jax.experimental import pallas as pl
from jax.experimental.pallas import tpu as pltpu
from jax.sharding import Mesh, PartitionSpec as P

HEAD_SIZE = 64
EXT = 80
VMEM_LIMIT = 24 * 2**20
SCORE = 2.5 / math.sqrt(HEAD_SIZE) * math.log2(math.e)
PLANE = ("xh", "y")
HEAD = ("xh", "y", "c")


def layer_norm(values):
    centered = values - jnp.mean(values, axis=-1, keepdims=True)
    return centered * lax.rsqrt(jnp.mean(centered * centered, axis=-1, keepdims=True) + 1e-05)


def column_norm(values):
    return values * lax.rsqrt(jnp.mean(values * values, axis=0, keepdims=True) + 1e-06)


def kernel_call(body, out_shape, name, flops, scratch=(), scalars=0, count=0):
    scalar = [pl.BlockSpec(memory_space=pltpu.SMEM)] * scalars
    return pl.pallas_call(
        body,
        in_specs=scalar + [pl.BlockSpec(memory_space=pltpu.VMEM)] * count,
        out_specs=jax.tree.map(lambda _: pl.BlockSpec(memory_space=pltpu.VMEM), out_shape),
        out_shape=out_shape,
        scratch_shapes=scratch,
        compiler_params=pltpu.CompilerParams(vmem_limit_bytes=VMEM_LIMIT),
        cost_estimate=pl.CostEstimate(flops=flops, transcendentals=0, bytes_accessed=2**20),
        name=name,
    )


def bf16(*shape):
    return jax.ShapeDtypeStruct(shape, jnp.bfloat16)


def ones_rows(count):
    row = lax.broadcasted_iota(jnp.int32, (EXT - HEAD_SIZE, count), 0)
    return jnp.where(row == 0, 1.0, 0.0).astype(jnp.bfloat16)


def times(rows, weight):
    return lax.dot_general(
        rows, weight, (((1,), (1,)), ((), ())), preferred_element_type=jnp.float32
    )


def project_kv_kernel(image_ref, weight_ref, both_ref, key_ref):
    product = times(image_ref[...], weight_ref[...]).T
    keys = column_norm(product[:HEAD_SIZE]).astype(jnp.bfloat16)
    both_ref[:HEAD_SIZE] = keys
    both_ref[HEAD_SIZE:] = product[HEAD_SIZE:].astype(jnp.bfloat16)
    key_ref[...] = keys.T


def project_kv(image_tokens, weight):
    rows, features = image_tokens.shape
    block = 512
    return pl.pallas_call(
        project_kv_kernel,
        grid=(rows // block,),
        in_specs=[
            pl.BlockSpec((block, features), lambda i: (i, 0)),
            pl.BlockSpec(weight.shape, lambda i: (0, 0)),
        ],
        out_specs=[
            pl.BlockSpec((2 * HEAD_SIZE, block), lambda i: (0, i)),
            pl.BlockSpec((block, HEAD_SIZE), lambda i: (i, 0)),
        ],
        out_shape=[bf16(2 * HEAD_SIZE, rows), bf16(rows, HEAD_SIZE)],
        compiler_params=pltpu.CompilerParams(vmem_limit_bytes=VMEM_LIMIT),
        cost_estimate=pl.CostEstimate(
            flops=6 * 10**9, transcendentals=0, bytes_accessed=rows * features * 2
        ),
        name="project_kv",
    )(image_tokens, weight)


def prepare_kernel(both_ref, key_ref):
    key_ref[...] = both_ref[:HEAD_SIZE].T


def prepare(both):
    return kernel_call(
        prepare_kernel, bf16(both.shape[1], HEAD_SIZE), "prepare", 10**9, count=1
    )(both)


def attend(queries, keys, both, step):
    total = jnp.zeros((EXT, queries.shape[1]), jnp.float32)
    ones = ones_rows(step)
    for first in range(0, keys.shape[0], step):
        scores = jnp.dot(
            keys[first : first + step, :], queries, preferred_element_type=jnp.float32
        )
        weights = jnp.exp2(scores).astype(jnp.bfloat16)
        values = jnp.concatenate([both[HEAD_SIZE:, first : first + step], ones], axis=0)
        total = total + jnp.dot(values, weights, preferred_element_type=jnp.float32)
    return total


def cross_kernel(query_count, carried, step, *refs):
    queries = [ref[...] for ref in refs[:query_count]]
    keys, both, *rest = refs[query_count:]
    together = queries[0] if query_count == 1 else jnp.concatenate(queries, axis=1)
    total = attend(together, keys, both, step)
    width = queries[0].shape[1]
    outs = rest[query_count:] if carried else rest
    for i, out in enumerate(outs):
        part = total[:, i * width : (i + 1) * width]
        if carried:
            part = part + rest[i][...]
        out[...] = part.astype(out.dtype)


def cross_attention(queries, piece, carried=None):
    width = queries[0].shape[1]
    count = len(queries)
    kind = jnp.float32 if carried is None else jnp.bfloat16
    extra = [] if carried is None else carried
    return kernel_call(
        functools.partial(cross_kernel, count, carried is not None, 1024 if count == 1 else 512),
        [jax.ShapeDtypeStruct((EXT, width), kind)] * count,
        "cross_attention",
        16 * HEAD_SIZE * width * count * piece[0].shape[0],
        count=count + 2 + len(extra),
    )(*queries, *piece, *extra)


def self_kernel(query_count, piece_count, carried, *refs):
    queries = jnp.concatenate([ref[...] for ref in refs[:query_count]], axis=1)
    pieces = refs[query_count : query_count + piece_count]
    rest = refs[query_count + piece_count :]
    outs = rest[query_count:] if carried else rest
    width = pieces[0].shape[1]
    total = jnp.zeros((EXT, queries.shape[1]), jnp.float32)
    for piece in pieces:
        total = total + attend(queries, piece[:HEAD_SIZE].T, piece, width)
    for i, out in enumerate(outs):
        part = total[:, i * width : (i + 1) * width]
        if carried:
            part = part + rest[i][...]
        out[...] = part.astype(out.dtype)


def self_attention(queries, pieces, carried=None, kind=jnp.float32):
    width = queries[0].shape[1]
    count = len(queries)
    extra = [] if carried is None else carried
    return kernel_call(
        functools.partial(self_kernel, count, len(pieces), carried is not None),
        [jax.ShapeDtypeStruct((EXT, width), kind)] * count,
        "self_attention",
        16 * HEAD_SIZE * width * count * width * len(pieces),
        count=count + len(pieces) + len(extra),
    )(*queries, *pieces, *extra)


def finish_kernel(slots, *refs):
    out_ref = refs[-1]
    total = functools.reduce(
        lambda x, y: x + y, [ref[...].astype(jnp.float32) for ref in refs[:-1]]
    )
    mix = (total[:HEAD_SIZE] / total[HEAD_SIZE : HEAD_SIZE + 1]).astype(jnp.bfloat16)
    width = out_ref.shape[2]
    for i in range(out_ref.shape[0]):
        first = (i % slots) * width
        out_ref[i] = mix[:, first : first + width]


def finish(partials, copies, slots):
    width = partials[0].shape[-1] // slots
    return kernel_call(
        functools.partial(finish_kernel, slots),
        bf16(copies, HEAD_SIZE, width),
        "finish",
        10**8,
        count=len(partials),
    )(*partials)


def place_heads(target, core, mine, other):
    plane, size, _ = mine.shape
    for i in range(plane):
        first = pl.multiple_of((2 * i + core) * size, size)
        target[pl.ds(first, size), :] = mine[i]
        first = pl.multiple_of((2 * i + 1 - core) * size, size)
        target[pl.ds(first, size), :] = other[i]


def place_rows(target, core, mine, other):
    plane, size, _ = mine.shape
    for i in range(plane):
        first = pl.multiple_of((plane * core + i) * size, size)
        target[pl.ds(first, size), :] = mine[i]
        first = pl.multiple_of((plane * (1 - core) + i) * size, size)
        target[pl.ds(first, size), :] = other[i]


def first_kernel(core_ref, mine_ref, other_ref, weight_ref, query_ref, rows):
    place_rows(rows, core_ref[0], mine_ref, other_ref)
    normed = layer_norm(rows[...].astype(jnp.float32)).astype(jnp.bfloat16)
    product = times(normed, weight_ref[...]).T
    query_ref[...] = (column_norm(product) * SCORE).astype(jnp.bfloat16)


def first_stage(core, mine, other, weight):
    plane, size, width = mine.shape
    rows = 2 * plane * size
    return kernel_call(
        first_kernel,
        bf16(HEAD_SIZE, rows),
        "first_stage",
        10**9,
        [pltpu.VMEM((rows, width), jnp.bfloat16)],
        scalars=1,
        count=3,
    )(core, mine, other, weight)


def middle_kernel(
    core_ref, mine_ref, other_ref, out_w, tri_mine, tri_other, qkv_w,
    stream_ref, query_ref, kv_ref, mix, rows, whole,
):
    core = core_ref[0]
    place_heads(mix, core, mine_ref, other_ref)
    place_rows(rows, core, tri_mine, tri_other)
    stream = rows[...].astype(jnp.float32) + jnp.dot(
        mix[...].T, out_w[...], preferred_element_type=jnp.float32
    )
    whole[...] = stream
    half = stream_ref.shape[0]
    stream_ref[...] = whole[pl.ds(pl.multiple_of(core * half, half), half), :]
    normed = layer_norm(stream).astype(jnp.bfloat16)
    product = times(normed, qkv_w[...]).T
    query_ref[...] = (column_norm(product[:HEAD_SIZE]) * SCORE).astype(jnp.bfloat16)
    kv_ref[:HEAD_SIZE] = column_norm(product[HEAD_SIZE : 2 * HEAD_SIZE]).astype(jnp.bfloat16)
    kv_ref[HEAD_SIZE:] = product[2 * HEAD_SIZE :].astype(jnp.bfloat16)


def middle_stage(core, mine, other, out_w, tri_parts, qkv_w):
    plane, size, width = tri_parts[0].shape
    count = 2 * plane * size
    return kernel_call(
        middle_kernel,
        [
            jax.ShapeDtypeStruct((plane * size, width), jnp.float32),
            bf16(HEAD_SIZE, count),
            bf16(2 * HEAD_SIZE, count),
        ],
        "middle_stage",
        3 * 10**9,
        [
            pltpu.VMEM((width, count), jnp.bfloat16),
            pltpu.VMEM((count, width), jnp.bfloat16),
            pltpu.VMEM((count, width), jnp.float32),
        ],
        scalars=1,
        count=6,
    )(core, mine, other, out_w, *tri_parts, qkv_w)


def last_kernel(
    place_ref, mix_ref, out_w, stream_ref, in_w, in_other, down_w, down_other,
    own_ref, part_ref, rows,
):
    plane, size, width = part_ref.shape
    stream = stream_ref[...] + jnp.dot(
        mix_ref[...].T, out_w[...], preferred_element_type=jnp.float32
    )
    rows[...] = stream
    own_ref[...] = rows[pl.ds(pl.multiple_of(place_ref[1] * size, size), size), :]
    normed = layer_norm(stream).astype(jnp.bfloat16)
    total = jnp.zeros(stream.shape, jnp.float32)
    for up, down in ((in_w, down_w), (in_other, down_other)):
        hidden = jax.nn.gelu(
            jnp.dot(normed, up[...], preferred_element_type=jnp.float32), approximate=True
        ).astype(jnp.bfloat16)
        total = total + jnp.dot(hidden, down[...], preferred_element_type=jnp.float32)
    for i in range(plane):
        part_ref[i] = total[i * size : (i + 1) * size].astype(jnp.bfloat16)


def last_stage(place, mix, out_w, stream, in_w, in_other, down_w, down_other, size):
    count, width = stream.shape
    return kernel_call(
        last_kernel,
        [jax.ShapeDtypeStruct((size, width), jnp.float32), bf16(count // size, size, width)],
        "last_stage",
        4 * 10**9,
        [pltpu.VMEM((count, width), jnp.float32)],
        scalars=1,
        count=7,
    )(place, mix, out_w, stream, in_w, in_other, down_w, down_other)


def exchange(values, axes):
    return lax.all_to_all(values, axes, 0, 0, tiled=True)


def copies_of(values, count):
    return jnp.broadcast_to(values, (count,) + values.shape)


def other_core(values):
    return lax.ppermute(values, "c", [(0, 1), (1, 0)])


def swap_near(values):
    return lax.ppermute(values, "xl", [(0, 1), (1, 0)])


def gather_head(copies):
    mine = exchange(copies, PLANE)
    return mine, other_core(mine)


def per_device(
    sizes,
    tri_tokens,
    image_tokens,
    cross_q,
    cross_kv,
    cross_out,
    self_qkv,
    self_out,
    mlp_in,
    mlp_out,
):
    size, width = tri_tokens.shape
    plane = sizes["xh"] * sizes["y"]
    z_axes = ("zh", "zl")
    z_count = sizes["zh"] * sizes["zl"]

    def along(values, shift):
        return lax.ppermute(values, z_axes, [(i, (i + shift) % z_count) for i in range(z_count)])

    core = jnp.stack([lax.axis_index("c"), lax.axis_index(PLANE)]).astype(jnp.int32)
    cross_out_all = lax.all_gather(cross_out, HEAD, axis=0, tiled=True)
    self_out_all = lax.all_gather(self_out, HEAD, axis=0, tiled=True)

    mine = exchange(copies_of(tri_tokens, plane), PLANE)
    kv_weight = jnp.swapaxes(cross_kv, 1, 2).reshape(-1, width)
    both, keys = project_kv(image_tokens, kv_weight)
    mine, both = lax.optimization_barrier((mine, both))
    other = other_core(mine)
    near = (keys, both)
    tri_parts = (mine, other)
    own = first_stage(core, mine, other, cross_q.T)

    def behind(value, done):
        return value if done is None else lax.optimization_barrier((value, done))[0]

    arrived = {0: own}
    sums = {None: None}

    def relay(block, shift, done):
        arrived[block - shift] = along(behind(arrived[block], sums[done]), shift)

    def near_part(block, done):
        (sums[block],) = cross_attention([behind(arrived[block], sums[done])], near)

    relay(0, 1, None)
    near_part(0, None)
    relay(0, -1, 0)
    relay(-1, 1, 0)
    near_part(-1, 0)
    relay(1, -1, -1)
    near_part(1, -1)
    relay(-2, 1, 1)
    near_part(-2, 1)
    relay(2, -1, -2)
    near_part(2, -2)
    relay(-3, 1, 2)
    near_part(-3, 2)
    near_part(3, -3)
    near_part(-4, 3)
    swapped = behind(swap_near(both), sums[3])
    far = (prepare(swapped), swapped)
    returned = []
    last = None
    for place, block in enumerate((-4, -3, 3, -2, 2, -1, 1, 0)):
        query = behind(arrived[block], last)
        if block == -1:
            query, cross_out_all = lax.optimization_barrier((query, cross_out_all))
        if place >= 6:
            query, returned[place - 6] = lax.optimization_barrier((query, returned[place - 6]))
        (last,) = cross_attention([query], far, [sums[block]])
        returned.append(along(last, block) if block else last)
    partials = returned
    mine, other = gather_head(finish(partials, plane, 1))
    self_weight = jnp.swapaxes(self_qkv, 1, 2).reshape(-1, width)
    stream, own, own_kv = middle_stage(
        core, mine, other, cross_out_all, tri_parts, self_weight
    )

    own, self_out_all = lax.optimization_barrier((own, self_out_all))
    (held_in, held_down), _ = lax.optimization_barrier(((mlp_in, mlp_out), sums[3]))
    in_other, down_other = other_core(held_in), other_core(held_down)
    left, right = along(own_kv, 1), along(own_kv, -1)
    queries = [own, swap_near(own)]
    carried = self_attention(queries, [own_kv])
    for step in range(3):
        blocks = [left, right]
        held, carried = lax.optimization_barrier((blocks, carried))
        left = along(held[0], 1)
        if step < 2:
            right = along(held[1], -1)
        carried = self_attention(queries, blocks, carried)
    here, there = self_attention(queries, [left], carried, jnp.bfloat16)
    slots = finish([here, swap_near(there)], plane * sizes["c"], sizes["c"])
    mix = exchange(slots, HEAD).reshape(width, plane * size)
    own, part = last_stage(
        core, mix, self_out_all, stream, mlp_in, in_other, mlp_out, down_other, size
    )
    collected = jnp.sum(exchange(part, PLANE).astype(jnp.float32), axis=0)
    return (own + collected).astype(jnp.bfloat16)


def solution(mesh):
    sizes = {"zh": 2, "zl": 4, "xl": 2, "xh": 2, "y": 4, "c": 2}
    names = tuple(sizes)
    fine = Mesh(mesh.devices.reshape(tuple(sizes.values())), names)
    tok = ("zh", "zl", "xl")
    return jax.shard_map(
        functools.partial(per_device, sizes),
        mesh=fine,
        in_specs=(
            P(names, None),
            P(tok, None),
            P(None, HEAD),
            P(None, None, HEAD),
            P(HEAD, None),
            P(None, None, HEAD),
            P(HEAD, None),
            P(None, HEAD),
            P(HEAD, None),
        ),
        out_specs=P(names, None),
        check_vma=False,
    )
```

```python
import functools
import math

import jax
import jax.numpy as jnp
from jax import lax
from jax.experimental import pallas as pl
from jax.experimental.pallas import tpu as pltpu
from jax.sharding import Mesh, PartitionSpec as P

HEAD_SIZE = 64
EXT = 80
VMEM_LIMIT = 16 * 2**20
SCORE = 2.5 / math.sqrt(HEAD_SIZE) * math.log2(math.e)
PLANE = ("xh", "y")
HEAD = ("xh", "y", "c")


def layer_norm(values):
    centered = values - jnp.mean(values, axis=-1, keepdims=True)
    return centered * lax.rsqrt(jnp.mean(centered * centered, axis=-1, keepdims=True) + 1e-05)


def column_norm(values):
    return values * lax.rsqrt(jnp.mean(values * values, axis=0, keepdims=True) + 1e-06)


def kernel_call(body, out_shape, name, flops, scratch=(), scalars=0, count=0):
    scalar = [pl.BlockSpec(memory_space=pltpu.SMEM)] * scalars
    return pl.pallas_call(
        body,
        in_specs=scalar + [pl.BlockSpec(memory_space=pltpu.VMEM)] * count,
        out_specs=jax.tree.map(lambda _: pl.BlockSpec(memory_space=pltpu.VMEM), out_shape),
        out_shape=out_shape,
        scratch_shapes=scratch,
        compiler_params=pltpu.CompilerParams(vmem_limit_bytes=VMEM_LIMIT),
        cost_estimate=pl.CostEstimate(flops=flops, transcendentals=0, bytes_accessed=2**20),
        name=name,
    )


def bf16(*shape):
    return jax.ShapeDtypeStruct(shape, jnp.bfloat16)


def ones_rows(count):
    row = lax.broadcasted_iota(jnp.int32, (EXT - HEAD_SIZE, count), 0)
    return jnp.where(row == 0, 1.0, 0.0).astype(jnp.bfloat16)


def times(rows, weight):
    return lax.dot_general(
        rows, weight, (((1,), (1,)), ((), ())), preferred_element_type=jnp.float32
    )


def project_kv_kernel(image_ref, weight_ref, both_ref):
    product = times(image_ref[...], weight_ref[...]).T
    both_ref[:HEAD_SIZE] = column_norm(product[:HEAD_SIZE]).astype(jnp.bfloat16)
    both_ref[HEAD_SIZE:] = product[HEAD_SIZE:].astype(jnp.bfloat16)


def project_kv(image_tokens, weight):
    rows, features = image_tokens.shape
    block = 512
    return pl.pallas_call(
        project_kv_kernel,
        grid=(rows // block,),
        in_specs=[
            pl.BlockSpec((block, features), lambda i: (i, 0)),
            pl.BlockSpec(weight.shape, lambda i: (0, 0)),
        ],
        out_specs=pl.BlockSpec((2 * HEAD_SIZE, block), lambda i: (0, i)),
        out_shape=bf16(2 * HEAD_SIZE, rows),
        compiler_params=pltpu.CompilerParams(vmem_limit_bytes=VMEM_LIMIT),
        cost_estimate=pl.CostEstimate(
            flops=6 * 10**9, transcendentals=0, bytes_accessed=rows * features * 2
        ),
        name="project_kv",
    )(image_tokens, weight)


def prepare_kernel(both_ref, key_ref):
    key_ref[...] = both_ref[:HEAD_SIZE].T


def prepare(both):
    return kernel_call(
        prepare_kernel, bf16(both.shape[1], HEAD_SIZE), "prepare", 10**9, count=1
    )(both)


def attend(queries, keys, both, step):
    total = jnp.zeros((EXT, queries.shape[1]), jnp.float32)
    ones = ones_rows(step)
    for first in range(0, keys.shape[0], step):
        scores = jnp.dot(
            keys[first : first + step, :], queries, preferred_element_type=jnp.float32
        )
        weights = jnp.exp2(scores).astype(jnp.bfloat16)
        values = jnp.concatenate([both[HEAD_SIZE:, first : first + step], ones], axis=0)
        total = total + jnp.dot(values, weights, preferred_element_type=jnp.float32)
    return total


def cross_kernel(step, query_ref, key_ref, both_ref, *refs):
    total = attend(query_ref[...], key_ref, both_ref, step)
    for extra in refs[:-1]:
        total = total + extra[...].astype(jnp.float32)
    refs[-1][...] = total.astype(refs[-1].dtype)


def cross_attention(query, piece, extras, kind):
    width = query.shape[1]
    return kernel_call(
        functools.partial(cross_kernel, 1024),
        jax.ShapeDtypeStruct((EXT, width), kind),
        "cross_attention",
        16 * HEAD_SIZE * width * piece[0].shape[0],
        count=3 + len(extras),
    )(query, *piece, *extras)


def self_kernel(query_count, piece_count, carried, *refs):
    queries = jnp.concatenate([ref[...] for ref in refs[:query_count]], axis=1)
    pieces = refs[query_count : query_count + piece_count]
    rest = refs[query_count + piece_count :]
    outs = rest[query_count:] if carried else rest
    width = pieces[0].shape[1]
    total = jnp.zeros((EXT, queries.shape[1]), jnp.float32)
    for piece in pieces:
        total = total + attend(queries, piece[:HEAD_SIZE].T, piece, width)
    for i, out in enumerate(outs):
        part = total[:, i * width : (i + 1) * width]
        if carried:
            part = part + rest[i][...]
        out[...] = part.astype(out.dtype)


def self_attention(queries, pieces, carried=None, kind=jnp.float32):
    width = queries[0].shape[1]
    count = len(queries)
    extra = [] if carried is None else carried
    return kernel_call(
        functools.partial(self_kernel, count, len(pieces), carried is not None),
        [jax.ShapeDtypeStruct((EXT, width), kind)] * count,
        "self_attention",
        16 * HEAD_SIZE * width * count * width * len(pieces),
        count=count + len(pieces) + len(extra),
    )(*queries, *pieces, *extra)


def finish_kernel(slots, *refs):
    out_ref = refs[-1]
    total = functools.reduce(
        lambda x, y: x + y, [ref[...].astype(jnp.float32) for ref in refs[:-1]]
    )
    mix = (total[:HEAD_SIZE] / total[HEAD_SIZE : HEAD_SIZE + 1]).astype(jnp.bfloat16)
    width = out_ref.shape[2]
    for i in range(out_ref.shape[0]):
        first = (i % slots) * width
        out_ref[i] = mix[:, first : first + width]


def finish(partials, copies, slots):
    width = partials[0].shape[-1] // slots
    return kernel_call(
        functools.partial(finish_kernel, slots),
        bf16(copies, HEAD_SIZE, width),
        "finish",
        10**8,
        count=len(partials),
    )(*partials)


def place_heads(target, core, mine, other):
    plane, size, _ = mine.shape
    for i in range(plane):
        first = pl.multiple_of((2 * i + core) * size, size)
        target[pl.ds(first, size), :] = mine[i]
        first = pl.multiple_of((2 * i + 1 - core) * size, size)
        target[pl.ds(first, size), :] = other[i]


def place_rows(target, core, mine, other):
    plane, size, _ = mine.shape
    for i in range(plane):
        first = pl.multiple_of((plane * core + i) * size, size)
        target[pl.ds(first, size), :] = mine[i]
        first = pl.multiple_of((plane * (1 - core) + i) * size, size)
        target[pl.ds(first, size), :] = other[i]


def first_kernel(core_ref, mine_ref, other_ref, weight_ref, query_ref, rows):
    place_rows(rows, core_ref[0], mine_ref, other_ref)
    normed = layer_norm(rows[...].astype(jnp.float32)).astype(jnp.bfloat16)
    product = times(normed, weight_ref[...]).T
    query_ref[...] = (column_norm(product) * SCORE).astype(jnp.bfloat16)


def first_stage(core, mine, other, weight):
    plane, size, width = mine.shape
    rows = 2 * plane * size
    return kernel_call(
        first_kernel,
        bf16(HEAD_SIZE, rows),
        "first_stage",
        10**9,
        [pltpu.VMEM((rows, width), jnp.bfloat16)],
        scalars=1,
        count=3,
    )(core, mine, other, weight)


def middle_kernel(
    core_ref, mine_ref, other_ref, out_w, tri_mine, tri_other, qkv_w,
    stream_ref, query_ref, kv_ref, mix, rows, whole,
):
    core = core_ref[0]
    place_heads(mix, core, mine_ref, other_ref)
    place_rows(rows, core, tri_mine, tri_other)
    stream = rows[...].astype(jnp.float32) + jnp.dot(
        mix[...].T, out_w[...], preferred_element_type=jnp.float32
    )
    whole[...] = stream
    half = stream_ref.shape[0]
    stream_ref[...] = whole[pl.ds(pl.multiple_of(core * half, half), half), :]
    normed = layer_norm(stream).astype(jnp.bfloat16)
    product = times(normed, qkv_w[...]).T
    query_ref[...] = (column_norm(product[:HEAD_SIZE]) * SCORE).astype(jnp.bfloat16)
    kv_ref[:HEAD_SIZE] = column_norm(product[HEAD_SIZE : 2 * HEAD_SIZE]).astype(jnp.bfloat16)
    kv_ref[HEAD_SIZE:] = product[2 * HEAD_SIZE :].astype(jnp.bfloat16)


def middle_stage(core, mine, other, out_w, tri_parts, qkv_w):
    plane, size, width = tri_parts[0].shape
    count = 2 * plane * size
    return kernel_call(
        middle_kernel,
        [
            jax.ShapeDtypeStruct((plane * size, width), jnp.float32),
            bf16(HEAD_SIZE, count),
            bf16(2 * HEAD_SIZE, count),
        ],
        "middle_stage",
        3 * 10**9,
        [
            pltpu.VMEM((width, count), jnp.bfloat16),
            pltpu.VMEM((count, width), jnp.bfloat16),
            pltpu.VMEM((count, width), jnp.float32),
        ],
        scalars=1,
        count=6,
    )(core, mine, other, out_w, *tri_parts, qkv_w)


def last_kernel(
    place_ref, mix_ref, out_w, stream_ref, in_w, in_other, down_w, down_other,
    own_ref, part_ref, rows,
):
    plane, size, width = part_ref.shape
    stream = stream_ref[...] + jnp.dot(
        mix_ref[...].T, out_w[...], preferred_element_type=jnp.float32
    )
    rows[...] = stream
    own_ref[...] = rows[pl.ds(pl.multiple_of(place_ref[1] * size, size), size), :]
    normed = layer_norm(stream).astype(jnp.bfloat16)
    total = jnp.zeros(stream.shape, jnp.float32)
    for up, down in ((in_w, down_w), (in_other, down_other)):
        hidden = jax.nn.gelu(
            jnp.dot(normed, up[...], preferred_element_type=jnp.float32), approximate=True
        ).astype(jnp.bfloat16)
        total = total + jnp.dot(hidden, down[...], preferred_element_type=jnp.float32)
    for i in range(plane):
        part_ref[i] = total[i * size : (i + 1) * size].astype(jnp.bfloat16)


def last_stage(place, mix, out_w, stream, in_w, in_other, down_w, down_other, size):
    count, width = stream.shape
    return kernel_call(
        last_kernel,
        [jax.ShapeDtypeStruct((size, width), jnp.float32), bf16(count // size, size, width)],
        "last_stage",
        4 * 10**9,
        [pltpu.VMEM((count, width), jnp.float32)],
        scalars=1,
        count=7,
    )(place, mix, out_w, stream, in_w, in_other, down_w, down_other)


def exchange(values, axes):
    return lax.all_to_all(values, axes, 0, 0, tiled=True)


def copies_of(values, count):
    return jnp.broadcast_to(values, (count,) + values.shape)


def other_core(values):
    return lax.ppermute(values, "c", [(0, 1), (1, 0)])


def swap_near(values):
    return lax.ppermute(values, "xl", [(0, 1), (1, 0)])


def gather_head(copies):
    mine = exchange(copies, PLANE)
    return mine, other_core(mine)


def per_device(
    sizes,
    tri_tokens,
    image_tokens,
    cross_q,
    cross_kv,
    cross_out,
    self_qkv,
    self_out,
    mlp_in,
    mlp_out,
):
    size, width = tri_tokens.shape
    plane = sizes["xh"] * sizes["y"]
    z_axes = ("zh", "zl")
    z_count = sizes["zh"] * sizes["zl"]

    def along(values, shift):
        return lax.ppermute(values, z_axes, [(i, (i + shift) % z_count) for i in range(z_count)])

    core = jnp.stack([lax.axis_index("c"), lax.axis_index(PLANE)]).astype(jnp.int32)
    tri_tokens, core = lax.optimization_barrier((tri_tokens, core))
    mine = exchange(copies_of(tri_tokens, plane), PLANE)
    both = project_kv(image_tokens, jnp.swapaxes(cross_kv, 1, 2).reshape(-1, width))
    mine, both, cross_out, self_out = lax.optimization_barrier((mine, both, cross_out, self_out))
    cross_out_all = lax.all_gather(cross_out, HEAD, axis=0, tiled=True)
    self_out_all = lax.all_gather(self_out, HEAD, axis=0, tiled=True)
    other = other_core(mine)
    near = (prepare(both), both)
    tri_parts = (mine, other)
    own = first_stage(core, mine, other, cross_q.T)

    def behind(value, done):
        return value if done is None else lax.optimization_barrier((value, done))[0]

    arrived = {0: own}
    sums = {None: None}

    def relay(block, shift, done):
        arrived[block - shift] = along(behind(arrived[block], sums[done]), shift)

    def near_part(block, done):
        sums[block] = cross_attention(behind(arrived[block], sums[done]), near, [], jnp.float32)

    relay(0, 1, None)
    near_part(0, None)
    relay(0, -1, 0)
    relay(-1, 1, 0)
    near_part(-1, 0)
    relay(1, -1, -1)
    near_part(1, -1)
    relay(-2, 1, 1)
    near_part(-2, 1)
    relay(2, -1, -2)
    near_part(2, -2)
    relay(-3, 1, 2)
    near_part(-3, 2)
    near_part(3, -3)
    swapped = behind(swap_near(both), sums[3])
    far = (prepare(swapped), swapped)
    passed = {}
    last = sums[3]
    for block in (3, -4, 2, -3, 1, -2, -1, 0):
        if block == -4:
            waiting = behind(arrived[-4], last)
            sums[-4] = cross_attention(waiting, near, [], jnp.float32)
            last = sums[-4]
        query = behind(arrived[block], last)
        extras = [sums[block]]
        if block in passed:
            extras.append(passed[block])
        if block == 0:
            break
        last = cross_attention(query, far, extras, jnp.bfloat16)
        step = 1 if block > 0 else -1
        sent = along(last, step)
        if block == step:
            passed[0, step] = sent
        else:
            passed[block - step] = sent
    home = cross_attention(query, far, extras, jnp.bfloat16)
    slots = finish([home, passed[0, 1], passed[0, -1]], plane, 1)
    slots, cross_out_all = lax.optimization_barrier((slots, cross_out_all))
    mine, other = gather_head(slots)
    self_weight = jnp.swapaxes(self_qkv, 1, 2).reshape(-1, width)
    stream, own, own_kv = middle_stage(
        core, mine, other, cross_out_all, tri_parts, self_weight
    )

    (held_in, held_down), _ = lax.optimization_barrier(((mlp_in, mlp_out), sums[3]))
    in_other, down_other = other_core(held_in), other_core(held_down)
    blocks, near_query = [along(own_kv, 1), along(own_kv, -1)], swap_near(own)
    blocks, near_query = lax.optimization_barrier((blocks, near_query))
    queries = [own, near_query]
    carried, waiting = None, [own_kv]
    for step in range(3):
        held = blocks
        if carried is not None:
            held, carried = lax.optimization_barrier((blocks, carried))
        blocks = [along(held[0], 1)]
        if step < 2:
            blocks.append(along(held[1], -1))
        carried = self_attention(queries, waiting, carried)
        waiting = held
    waiting, carried, self_out_all = lax.optimization_barrier(
        (waiting + blocks, carried, self_out_all)
    )
    here, there = self_attention(queries, waiting, carried, jnp.bfloat16)
    slots = finish([here, swap_near(there)], plane * sizes["c"], sizes["c"])
    mix = exchange(slots, HEAD).reshape(width, plane * size)
    own, part = last_stage(
        core, mix, self_out_all, stream, mlp_in, in_other, mlp_out, down_other, size
    )
    collected = jnp.sum(exchange(part, PLANE).astype(jnp.float32), axis=0)
    return (own + collected).astype(jnp.bfloat16)


def solution(mesh):
    sizes = {"zh": 2, "zl": 4, "xl": 2, "xh": 2, "y": 4, "c": 2}
    names = tuple(sizes)
    fine = Mesh(mesh.devices.reshape(tuple(sizes.values())), names)
    tok = ("zh", "zl", "xl")
    return jax.shard_map(
        functools.partial(per_device, sizes),
        mesh=fine,
        in_specs=(
            P(names, None),
            P(tok, None),
            P(None, HEAD),
            P(None, None, HEAD),
            P(HEAD, None),
            P(None, None, HEAD),
            P(HEAD, None),
            P(None, HEAD),
            P(HEAD, None),
        ),
        out_specs=P(names, None),
        check_vma=False,
    )
```

```python
import functools
import math

import jax
import jax.numpy as jnp
from jax import lax
from jax.experimental import pallas as pl
from jax.experimental.pallas import tpu as pltpu
from jax.sharding import Mesh, PartitionSpec as P

HEAD_SIZE = 64
EXT = 80
VMEM_LIMIT = 24 * 2**20
SCORE = 2.5 / math.sqrt(HEAD_SIZE) * math.log2(math.e)
PLANE = ("xh", "y")
HEAD = ("xh", "y", "c")


def layer_norm(values):
    centered = values - jnp.mean(values, axis=-1, keepdims=True)
    return centered * lax.rsqrt(jnp.mean(centered * centered, axis=-1, keepdims=True) + 1e-05)


def column_norm(values):
    return values * lax.rsqrt(jnp.mean(values * values, axis=0, keepdims=True) + 1e-06)


def kernel_call(body, out_shape, name, flops, scratch=(), scalars=0, count=0, aliases={}):
    scalar = [pl.BlockSpec(memory_space=pltpu.SMEM)] * scalars
    return pl.pallas_call(
        body,
        in_specs=scalar
        + [
            pl.BlockSpec(memory_space=pl.ANY if i + scalars in aliases else pltpu.VMEM)
            for i in range(count)
        ],
        input_output_aliases=aliases,
        out_specs=jax.tree.map(
            lambda shape: pl.BlockSpec(
                memory_space=pltpu.VMEM if isinstance(shape, jax.ShapeDtypeStruct) else pl.ANY
            ),
            out_shape,
        ),
        out_shape=out_shape,
        scratch_shapes=scratch,
        compiler_params=pltpu.CompilerParams(vmem_limit_bytes=VMEM_LIMIT),
        cost_estimate=pl.CostEstimate(flops=flops, transcendentals=0, bytes_accessed=2**20),
        name=name,
    )


def bf16(*shape):
    return jax.ShapeDtypeStruct(shape, jnp.bfloat16)


def ones_rows(count):
    row = lax.broadcasted_iota(jnp.int32, (EXT - HEAD_SIZE, count), 0)
    return jnp.where(row == 0, 1.0, 0.0).astype(jnp.bfloat16)


def times(rows, weight):
    return lax.dot_general(
        rows, weight, (((1,), (1,)), ((), ())), preferred_element_type=jnp.float32
    )


def project_kv_kernel(image_ref, weight_ref, both_ref):
    product = times(image_ref[...], weight_ref[...]).T
    both_ref[:HEAD_SIZE] = column_norm(product[:HEAD_SIZE]).astype(jnp.bfloat16)
    both_ref[HEAD_SIZE:] = product[HEAD_SIZE:].astype(jnp.bfloat16)


def project_kv(image_tokens, weight):
    rows, features = image_tokens.shape
    block = 512
    return pl.pallas_call(
        project_kv_kernel,
        grid=(rows // block,),
        in_specs=[
            pl.BlockSpec((block, features), lambda i: (i, 0)),
            pl.BlockSpec(weight.shape, lambda i: (0, 0)),
        ],
        out_specs=pl.BlockSpec((2 * HEAD_SIZE, block), lambda i: (0, i)),
        out_shape=bf16(2 * HEAD_SIZE, rows),
        compiler_params=pltpu.CompilerParams(vmem_limit_bytes=VMEM_LIMIT),
        cost_estimate=pl.CostEstimate(
            flops=6 * 10**9, transcendentals=0, bytes_accessed=rows * features * 2
        ),
        name="project_kv",
    )(image_tokens, weight)


def prepare_kernel(both_ref, key_ref):
    key_ref[...] = both_ref[:HEAD_SIZE].T


def prepare(both):
    return kernel_call(
        prepare_kernel, bf16(both.shape[1], HEAD_SIZE), "prepare", 10**9, count=1
    )(both)


def attend(queries, keys, both, step):
    total = jnp.zeros((EXT, queries.shape[1]), jnp.float32)
    ones = ones_rows(step)
    for first in range(0, keys.shape[0], step):
        scores = jnp.dot(
            keys[first : first + step, :], queries, preferred_element_type=jnp.float32
        )
        weights = jnp.exp2(scores).astype(jnp.bfloat16)
        values = jnp.concatenate([both[HEAD_SIZE:, first : first + step], ones], axis=0)
        total = total + jnp.dot(values, weights, preferred_element_type=jnp.float32)
    return total


def cross_kernel(step, query_ref, key_ref, both_ref, *refs):
    total = attend(query_ref[...], key_ref, both_ref, step)
    for extra in refs[:-1]:
        total = total + extra[...].astype(jnp.float32)
    refs[-1][...] = total.astype(refs[-1].dtype)


def cross_attention(query, piece, extras, kind):
    width = query.shape[1]
    return kernel_call(
        functools.partial(cross_kernel, 1024),
        jax.ShapeDtypeStruct((EXT, width), kind),
        "cross_attention",
        16 * HEAD_SIZE * width * piece[0].shape[0],
        count=3 + len(extras),
    )(query, *piece, *extras)


def self_kernel(query_count, piece_count, carried, *refs):
    queries = jnp.concatenate([ref[...] for ref in refs[:query_count]], axis=1)
    pieces = refs[query_count : query_count + piece_count]
    rest = refs[query_count + piece_count :]
    outs = rest[query_count:] if carried else rest
    width = pieces[0].shape[1]
    total = jnp.zeros((EXT, queries.shape[1]), jnp.float32)
    for piece in pieces:
        total = total + attend(queries, piece[:HEAD_SIZE].T, piece, width)
    for i, out in enumerate(outs):
        part = total[:, i * width : (i + 1) * width]
        if carried:
            part = part + rest[i][...]
        out[...] = part.astype(out.dtype)


def self_attention(queries, pieces, carried=None, kind=jnp.float32):
    width = queries[0].shape[1]
    count = len(queries)
    extra = [] if carried is None else carried
    return kernel_call(
        functools.partial(self_kernel, count, len(pieces), carried is not None),
        [jax.ShapeDtypeStruct((EXT, width), kind)] * count,
        "self_attention",
        16 * HEAD_SIZE * width * count * width * len(pieces),
        count=count + len(pieces) + len(extra),
    )(*queries, *pieces, *extra)


def finish_kernel(slots, *refs):
    out_ref = refs[-1]
    total = functools.reduce(
        lambda x, y: x + y, [ref[...].astype(jnp.float32) for ref in refs[:-1]]
    )
    mix = (total[:HEAD_SIZE] / total[HEAD_SIZE : HEAD_SIZE + 1]).astype(jnp.bfloat16)
    width = out_ref.shape[2]
    for i in range(out_ref.shape[0]):
        first = (i % slots) * width
        out_ref[i] = mix[:, first : first + width]


def finish(partials, copies, slots):
    width = partials[0].shape[-1] // slots
    return kernel_call(
        functools.partial(finish_kernel, slots),
        bf16(copies, HEAD_SIZE, width),
        "finish",
        10**8,
        count=len(partials),
    )(*partials)


def place_heads(target, core, mine, other):
    plane, size, _ = mine.shape
    for i in range(plane):
        first = pl.multiple_of((2 * i + core) * size, size)
        target[pl.ds(first, size), :] = mine[i]
        first = pl.multiple_of((2 * i + 1 - core) * size, size)
        target[pl.ds(first, size), :] = other[i]


def place_rows(target, core, mine, other):
    plane, size, _ = mine.shape
    for i in range(plane):
        first = pl.multiple_of((plane * core + i) * size, size)
        target[pl.ds(first, size), :] = mine[i]
        first = pl.multiple_of((plane * (1 - core) + i) * size, size)
        target[pl.ds(first, size), :] = other[i]


def first_kernel(core_ref, mine_ref, other_ref, weight_ref, query_ref, rows):
    place_rows(rows, core_ref[0], mine_ref, other_ref)
    normed = layer_norm(rows[...].astype(jnp.float32)).astype(jnp.bfloat16)
    product = times(normed, weight_ref[...]).T
    query_ref[...] = (column_norm(product) * SCORE).astype(jnp.bfloat16)


def first_stage(core, mine, other, weight):
    plane, size, width = mine.shape
    rows = 2 * plane * size
    return kernel_call(
        first_kernel,
        bf16(HEAD_SIZE, rows),
        "first_stage",
        10**9,
        [pltpu.VMEM((rows, width), jnp.bfloat16)],
        scalars=1,
        count=3,
    )(core, mine, other, weight)


FETCHES = 4


def fetch(source, target, sems):
    size = source.shape[0] // FETCHES
    copies = []
    for i in range(FETCHES):
        rows = pl.ds(i * size, size)
        copies.append(pltpu.make_async_copy(source.at[rows, :], target.at[rows, :], sems.at[i]))
        copies[-1].start()
    return copies


def fetched_product(left, target, copies):
    size = target.shape[0] // FETCHES
    total = None
    for i, copy in enumerate(copies):
        copy.wait()
        part = jnp.dot(
            left[:, i * size : (i + 1) * size],
            target[i * size : (i + 1) * size, :],
            preferred_element_type=jnp.float32,
        )
        total = part if total is None else total + part
    return total


def middle_kernel(
    core_ref, mine_ref, other_ref, out_w, tri_mine, tri_other, qkv_w,
    stream_ref, query_ref, kv_ref, _same_w, mix, rows, whole, sem, out_rows, sems,
):
    copies = fetch(out_w, out_rows, sems)
    core = core_ref[0]
    place_heads(mix, core, mine_ref, other_ref)
    place_rows(rows, core, tri_mine, tri_other)
    stream = rows[...].astype(jnp.float32) + fetched_product(mix[...].T, out_rows, copies)
    whole[...] = stream
    half = stream_ref.shape[0]
    copy = pltpu.make_async_copy(
        whole.at[pl.ds(pl.multiple_of(core * half, half), half), :], stream_ref, sem
    )
    copy.start()
    normed = layer_norm(stream).astype(jnp.bfloat16)
    product = times(normed, qkv_w[...]).T
    query_ref[...] = (column_norm(product[:HEAD_SIZE]) * SCORE).astype(jnp.bfloat16)
    kv_ref[:HEAD_SIZE] = column_norm(product[HEAD_SIZE : 2 * HEAD_SIZE]).astype(jnp.bfloat16)
    kv_ref[HEAD_SIZE:] = product[2 * HEAD_SIZE :].astype(jnp.bfloat16)
    copy.wait()


def middle_stage(core, mine, other, out_w, tri_parts, qkv_w):
    plane, size, width = tri_parts[0].shape
    count = 2 * plane * size
    return kernel_call(
        middle_kernel,
        [
            pltpu.HBM((plane * size, width), jnp.float32),
            bf16(HEAD_SIZE, count),
            bf16(2 * HEAD_SIZE, count),
            pltpu.HBM(out_w.shape, out_w.dtype),
        ],
        "middle_stage",
        3 * 10**9,
        [
            pltpu.VMEM((width, count), jnp.bfloat16),
            pltpu.VMEM((count, width), jnp.bfloat16),
            pltpu.VMEM((count, width), jnp.float32),
            pltpu.SemaphoreType.DMA,
            pltpu.VMEM(out_w.shape, jnp.bfloat16),
            pltpu.SemaphoreType.DMA((FETCHES,)),
        ],
        scalars=1,
        count=6,
        aliases={3: 3},
    )(core, mine, other, out_w, *tri_parts, qkv_w)[:3]


def last_kernel(
    place_ref, mix_ref, out_w, stream_ref, in_w, in_other, down_w, down_other,
    own_ref, part_ref, _same_w, _same_stream, rows, out_rows, sems, sem,
):
    copies = fetch(out_w, out_rows, sems)
    carry = pltpu.make_async_copy(stream_ref, rows, sem)
    carry.start()
    plane, size, width = part_ref.shape
    product = fetched_product(mix_ref[...].T, out_rows, copies)
    carry.wait()
    stream = rows[...] + product
    rows[...] = stream
    own_ref[...] = rows[pl.ds(pl.multiple_of(place_ref[1] * size, size), size), :]
    normed = layer_norm(stream).astype(jnp.bfloat16)
    total = jnp.zeros(stream.shape, jnp.float32)
    for up, down in ((in_w, down_w), (in_other, down_other)):
        hidden = jax.nn.gelu(
            jnp.dot(normed, up[...], preferred_element_type=jnp.float32), approximate=True
        ).astype(jnp.bfloat16)
        total = total + jnp.dot(hidden, down[...], preferred_element_type=jnp.float32)
    for i in range(plane):
        part_ref[i] = total[i * size : (i + 1) * size].astype(jnp.bfloat16)


def last_stage(place, mix, out_w, stream, in_w, in_other, down_w, down_other, size):
    count, width = stream.shape
    return kernel_call(
        last_kernel,
        [
            jax.ShapeDtypeStruct((size, width), jnp.float32),
            bf16(count // size, size, width),
            pltpu.HBM(out_w.shape, out_w.dtype),
            pltpu.HBM(stream.shape, stream.dtype),
        ],
        "last_stage",
        4 * 10**9,
        [
            pltpu.VMEM((count, width), jnp.float32),
            pltpu.VMEM(out_w.shape, jnp.bfloat16),
            pltpu.SemaphoreType.DMA((FETCHES,)),
            pltpu.SemaphoreType.DMA,
        ],
        scalars=1,
        count=7,
        aliases={2: 2, 3: 3},
    )(place, mix, out_w, stream, in_w, in_other, down_w, down_other)[:2]


def exchange(values, axes):
    return lax.all_to_all(values, axes, 0, 0, tiled=True)


def copies_kernel(value_ref, out_ref, sems):
    copies = [
        pltpu.make_async_copy(value_ref, out_ref.at[i], sems.at[i]) for i in range(out_ref.shape[0])
    ]
    for copy in copies:
        copy.start()
    for copy in copies:
        copy.wait()


def copies_of(values, count):
    return kernel_call(
        copies_kernel,
        pltpu.HBM((count,) + values.shape, values.dtype),
        "copies",
        10**7,
        [pltpu.SemaphoreType.DMA((count,))],
        count=1,
    )(values)


def other_core(values):
    return lax.ppermute(values, "c", [(0, 1), (1, 0)])


def swap_near(values):
    return lax.ppermute(values, "xl", [(0, 1), (1, 0)])


def gather_head(copies):
    mine = exchange(copies, PLANE)
    return mine, other_core(mine)


def per_device(
    sizes,
    tri_tokens,
    image_tokens,
    cross_q,
    cross_kv,
    cross_out,
    self_qkv,
    self_out,
    mlp_in,
    mlp_out,
):
    size, width = tri_tokens.shape
    plane = sizes["xh"] * sizes["y"]
    z_axes = ("zh", "zl")
    z_count = sizes["zh"] * sizes["zl"]

    def along(values, shift):
        return lax.ppermute(values, z_axes, [(i, (i + shift) % z_count) for i in range(z_count)])

    core = jnp.stack([lax.axis_index("c"), lax.axis_index(PLANE)]).astype(jnp.int32)
    tri_tokens, core = lax.optimization_barrier((tri_tokens, core))
    mine = exchange(copies_of(tri_tokens, plane), PLANE)
    both = project_kv(image_tokens, jnp.swapaxes(cross_kv, 1, 2).reshape(-1, width))
    mine, both, cross_out, self_out = lax.optimization_barrier((mine, both, cross_out, self_out))
    cross_out_all = lax.all_gather(cross_out, HEAD, axis=0, tiled=True)
    self_out_all = lax.all_gather(self_out, HEAD, axis=0, tiled=True)
    other = other_core(mine)
    near = (prepare(both), both)
    tri_parts = (mine, other)
    own = first_stage(core, mine, other, cross_q.T)

    def behind(value, done):
        return value if done is None else lax.optimization_barrier((value, done))[0]

    arrived = {0: own}
    sums = {None: None}

    def relay(block, shift, done):
        arrived[block - shift] = along(behind(arrived[block], sums[done]), shift)

    def near_part(block, done):
        sums[block] = cross_attention(behind(arrived[block], sums[done]), near, [], jnp.float32)

    relay(0, 1, None)
    near_part(0, None)
    relay(0, -1, 0)
    relay(-1, 1, 0)
    near_part(-1, 0)
    relay(1, -1, -1)
    near_part(1, -1)
    relay(-2, 1, 1)
    near_part(-2, 1)
    relay(2, -1, -2)
    near_part(2, -2)
    relay(-3, 1, 2)
    near_part(-3, 2)
    near_part(3, -3)
    swapped = behind(swap_near(both), sums[3])
    far = (prepare(swapped), swapped)
    passed = {}
    last = sums[3]
    for block in (3, -4, 2, -3, 1, -2, -1, 0):
        if block == -4:
            waiting = behind(arrived[-4], last)
            sums[-4] = cross_attention(waiting, near, [], jnp.float32)
            last = sums[-4]
        query = behind(arrived[block], last)
        extras = [sums[block]]
        if block in passed:
            extras.append(passed[block])
        if block == 0:
            break
        last = cross_attention(query, far, extras, jnp.bfloat16)
        step = 1 if block > 0 else -1
        sent = along(last, step)
        if block == step:
            passed[0, step] = sent
        else:
            passed[block - step] = sent
    home = cross_attention(query, far, extras, jnp.bfloat16)
    home, cross_out_all = lax.optimization_barrier((home, cross_out_all))
    slots = finish([home, passed[0, 1], passed[0, -1]], plane, 1)
    mine, other = gather_head(slots)
    self_weight = jnp.swapaxes(self_qkv, 1, 2).reshape(-1, width)
    stream, own, own_kv = middle_stage(
        core, mine, other, cross_out_all, tri_parts, self_weight
    )

    (held_in, held_down), _ = lax.optimization_barrier(((mlp_in, mlp_out), sums[3]))
    in_other, down_other = other_core(held_in), other_core(held_down)
    blocks, near_query = [along(own_kv, 1), along(own_kv, -1)], swap_near(own)
    blocks, near_query = lax.optimization_barrier((blocks, near_query))
    queries = [own, near_query]
    carried, waiting = None, [own_kv]
    for step in range(3):
        held = blocks
        if carried is not None:
            held, carried = lax.optimization_barrier((blocks, carried))
        blocks = [along(held[0], 1)]
        if step < 2:
            blocks.append(along(held[1], -1))
        carried = self_attention(queries, waiting, carried)
        waiting = held
    here, there = self_attention(queries, waiting + blocks, carried, jnp.bfloat16)
    there, self_out_all = lax.optimization_barrier((there, self_out_all))
    slots = finish([here, swap_near(there)], plane * sizes["c"], sizes["c"])
    mix = exchange(slots, HEAD).reshape(width, plane * size)
    own, part = last_stage(
        core, mix, self_out_all, stream, mlp_in, in_other, mlp_out, down_other, size
    )
    collected = jnp.sum(exchange(part, PLANE).astype(jnp.float32), axis=0)
    return (own + collected).astype(jnp.bfloat16)


def solution(mesh):
    sizes = {"zh": 2, "zl": 4, "xl": 2, "xh": 2, "y": 4, "c": 2}
    names = tuple(sizes)
    fine = Mesh(mesh.devices.reshape(tuple(sizes.values())), names)
    tok = ("zh", "zl", "xl")
    return jax.shard_map(
        functools.partial(per_device, sizes),
        mesh=fine,
        in_specs=(
            P(names, None),
            P(tok, None),
            P(None, HEAD),
            P(None, None, HEAD),
            P(HEAD, None),
            P(None, None, HEAD),
            P(HEAD, None),
            P(None, HEAD),
            P(HEAD, None),
        ),
        out_specs=P(names, None),
        check_vma=False,
    )
```

```python
import functools
import math

import jax
import jax.numpy as jnp
from jax import lax
from jax.experimental import pallas as pl
from jax.experimental.pallas import tpu as pltpu
from jax.sharding import Mesh, PartitionSpec as P

HEAD_SIZE = 64
EXT = 80
VMEM_LIMIT = 24 * 2**20
SCORE = 2.5 / math.sqrt(HEAD_SIZE) * math.log2(math.e)
PLANE = ("xh", "y")
HEAD = ("xh", "y", "c")


def layer_norm(values):
    centered = values - jnp.mean(values, axis=-1, keepdims=True)
    return centered * lax.rsqrt(jnp.mean(centered * centered, axis=-1, keepdims=True) + 1e-05)


def column_norm(values):
    return values * lax.rsqrt(jnp.mean(values * values, axis=0, keepdims=True) + 1e-06)


def kernel_call(body, out_shape, name, flops, scratch=(), scalars=0, count=0, aliases={}):
    scalar = [pl.BlockSpec(memory_space=pltpu.SMEM)] * scalars
    return pl.pallas_call(
        body,
        in_specs=scalar
        + [
            pl.BlockSpec(memory_space=pl.ANY if i + scalars in aliases else pltpu.VMEM)
            for i in range(count)
        ],
        input_output_aliases=aliases,
        out_specs=jax.tree.map(
            lambda shape: pl.BlockSpec(
                memory_space=pltpu.VMEM if isinstance(shape, jax.ShapeDtypeStruct) else pl.ANY
            ),
            out_shape,
        ),
        out_shape=out_shape,
        scratch_shapes=scratch,
        compiler_params=pltpu.CompilerParams(vmem_limit_bytes=VMEM_LIMIT),
        cost_estimate=pl.CostEstimate(flops=flops, transcendentals=0, bytes_accessed=2**20),
        name=name,
    )


def bf16(*shape):
    return jax.ShapeDtypeStruct(shape, jnp.bfloat16)


def ones_rows(count):
    row = lax.broadcasted_iota(jnp.int32, (EXT - HEAD_SIZE, count), 0)
    return jnp.where(row == 0, 1.0, 0.0).astype(jnp.bfloat16)


def times(rows, weight):
    return lax.dot_general(
        rows, weight, (((1,), (1,)), ((), ())), preferred_element_type=jnp.float32
    )


def project_kv_kernel(image_ref, weight_ref, both_ref):
    product = times(image_ref[...], weight_ref[...]).T
    both_ref[:HEAD_SIZE] = column_norm(product[:HEAD_SIZE]).astype(jnp.bfloat16)
    both_ref[HEAD_SIZE:] = product[HEAD_SIZE:].astype(jnp.bfloat16)


def project_kv(image_tokens, weight):
    rows, features = image_tokens.shape
    block = 512
    return pl.pallas_call(
        project_kv_kernel,
        grid=(rows // block,),
        in_specs=[
            pl.BlockSpec((block, features), lambda i: (i, 0)),
            pl.BlockSpec(weight.shape, lambda i: (0, 0)),
        ],
        out_specs=pl.BlockSpec((2 * HEAD_SIZE, block), lambda i: (0, i)),
        out_shape=bf16(2 * HEAD_SIZE, rows),
        compiler_params=pltpu.CompilerParams(vmem_limit_bytes=VMEM_LIMIT),
        cost_estimate=pl.CostEstimate(
            flops=6 * 10**9, transcendentals=0, bytes_accessed=rows * features * 2
        ),
        name="project_kv",
    )(image_tokens, weight)


def prepare_kernel(both_ref, key_ref):
    key_ref[...] = both_ref[:HEAD_SIZE].T


def prepare(both):
    return kernel_call(
        prepare_kernel, bf16(both.shape[1], HEAD_SIZE), "prepare", 10**9, count=1
    )(both)


def attend(queries, keys, both, step, ahead):
    total = jnp.zeros((EXT, queries.shape[1]), jnp.float32)
    ones = ones_rows(step)
    starts = list(range(0, keys.shape[0], step))

    def scores_of(first):
        return jnp.dot(
            keys[first : first + step, :], queries, preferred_element_type=jnp.float32
        )

    pending = [scores_of(first) for first in starts[:ahead]]
    for place, first in enumerate(starts):
        if place + ahead < len(starts):
            pending.append(scores_of(starts[place + ahead]))
        weights = jnp.exp2(pending.pop(0)).astype(jnp.bfloat16)
        values = jnp.concatenate([both[HEAD_SIZE:, first : first + step], ones], axis=0)
        total = total + jnp.dot(values, weights, preferred_element_type=jnp.float32)
    return total


def cross_kernel(step, query_ref, key_ref, both_ref, *refs):
    total = attend(query_ref[...], key_ref, both_ref, step, 3)
    for extra in refs[:-1]:
        total = total + extra[...].astype(jnp.float32)
    refs[-1][...] = total.astype(refs[-1].dtype)


def cross_attention(query, piece, extras, kind):
    width = query.shape[1]
    return kernel_call(
        functools.partial(cross_kernel, 256),
        jax.ShapeDtypeStruct((EXT, width), kind),
        "cross_attention",
        16 * HEAD_SIZE * width * piece[0].shape[0],
        count=3 + len(extras),
    )(query, *piece, *extras)


def self_kernel(query_count, piece_count, carried, *refs):
    queries = jnp.concatenate([ref[...] for ref in refs[:query_count]], axis=1)
    pieces = refs[query_count : query_count + piece_count]
    rest = refs[query_count + piece_count :]
    outs = rest[query_count:] if carried else rest
    width = pieces[0].shape[1]
    total = jnp.zeros((EXT, queries.shape[1]), jnp.float32)
    for piece in pieces:
        total = total + attend(queries, piece[:HEAD_SIZE].T, piece, width, 1)
    for i, out in enumerate(outs):
        part = total[:, i * width : (i + 1) * width]
        if carried:
            part = part + rest[i][...]
        out[...] = part.astype(out.dtype)


def self_attention(queries, pieces, carried=None, kind=jnp.float32):
    width = queries[0].shape[1]
    count = len(queries)
    extra = [] if carried is None else carried
    return kernel_call(
        functools.partial(self_kernel, count, len(pieces), carried is not None),
        [jax.ShapeDtypeStruct((EXT, width), kind)] * count,
        "self_attention",
        16 * HEAD_SIZE * width * count * width * len(pieces),
        count=count + len(pieces) + len(extra),
    )(*queries, *pieces, *extra)


def finish_kernel(slots, *refs):
    out_ref = refs[-1]
    total = functools.reduce(
        lambda x, y: x + y, [ref[...].astype(jnp.float32) for ref in refs[:-1]]
    )
    mix = (total[:HEAD_SIZE] / total[HEAD_SIZE : HEAD_SIZE + 1]).astype(jnp.bfloat16)
    width = out_ref.shape[2]
    for i in range(out_ref.shape[0]):
        first = (i % slots) * width
        out_ref[i] = mix[:, first : first + width]


def finish(partials, copies, slots):
    width = partials[0].shape[-1] // slots
    return kernel_call(
        functools.partial(finish_kernel, slots),
        bf16(copies, HEAD_SIZE, width),
        "finish",
        10**8,
        count=len(partials),
    )(*partials)


def place_heads(target, core, mine, other):
    plane, size, _ = mine.shape
    for i in range(plane):
        first = pl.multiple_of((2 * i + core) * size, size)
        target[pl.ds(first, size), :] = mine[i]
        first = pl.multiple_of((2 * i + 1 - core) * size, size)
        target[pl.ds(first, size), :] = other[i]


def place_rows(target, core, mine, other):
    plane, size, _ = mine.shape
    for i in range(plane):
        first = pl.multiple_of((plane * core + i) * size, size)
        target[pl.ds(first, size), :] = mine[i]
        first = pl.multiple_of((plane * (1 - core) + i) * size, size)
        target[pl.ds(first, size), :] = other[i]


def first_kernel(core_ref, mine_ref, other_ref, weight_ref, query_ref, rows):
    place_rows(rows, core_ref[0], mine_ref, other_ref)
    normed = layer_norm(rows[...].astype(jnp.float32)).astype(jnp.bfloat16)
    product = times(normed, weight_ref[...]).T
    query_ref[...] = (column_norm(product) * SCORE).astype(jnp.bfloat16)


def first_stage(core, mine, other, weight):
    plane, size, width = mine.shape
    rows = 2 * plane * size
    return kernel_call(
        first_kernel,
        bf16(HEAD_SIZE, rows),
        "first_stage",
        10**9,
        [pltpu.VMEM((rows, width), jnp.bfloat16)],
        scalars=1,
        count=3,
    )(core, mine, other, weight)


FETCHES = 4


def fetch(source, target, sems):
    size = source.shape[0] // FETCHES
    copies = []
    for i in range(FETCHES):
        rows = pl.ds(i * size, size)
        copies.append(pltpu.make_async_copy(source.at[rows, :], target.at[rows, :], sems.at[i]))
        copies[-1].start()
    return copies


def fetched_product(left, target, copies):
    size = target.shape[0] // FETCHES
    total = None
    for i, copy in enumerate(copies):
        copy.wait()
        part = jnp.dot(
            left[:, i * size : (i + 1) * size],
            target[i * size : (i + 1) * size, :],
            preferred_element_type=jnp.float32,
        )
        total = part if total is None else total + part
    return total


def middle_kernel(
    core_ref, mine_ref, other_ref, out_w, tri_mine, tri_other, qkv_w,
    stream_ref, query_ref, kv_ref, _same_w, mix, rows, whole, sem, out_rows, sems,
):
    copies = fetch(out_w, out_rows, sems)
    core = core_ref[0]
    place_heads(mix, core, mine_ref, other_ref)
    place_rows(rows, core, tri_mine, tri_other)
    stream = rows[...].astype(jnp.float32) + fetched_product(mix[...].T, out_rows, copies)
    whole[...] = stream
    half = stream_ref.shape[0]
    copy = pltpu.make_async_copy(
        whole.at[pl.ds(pl.multiple_of(core * half, half), half), :], stream_ref, sem
    )
    copy.start()
    normed = layer_norm(stream).astype(jnp.bfloat16)
    product = times(normed, qkv_w[...]).T
    query_ref[...] = (column_norm(product[:HEAD_SIZE]) * SCORE).astype(jnp.bfloat16)
    kv_ref[:HEAD_SIZE] = column_norm(product[HEAD_SIZE : 2 * HEAD_SIZE]).astype(jnp.bfloat16)
    kv_ref[HEAD_SIZE:] = product[2 * HEAD_SIZE :].astype(jnp.bfloat16)
    copy.wait()


def middle_stage(core, mine, other, out_w, tri_parts, qkv_w):
    plane, size, width = tri_parts[0].shape
    count = 2 * plane * size
    return kernel_call(
        middle_kernel,
        [
            pltpu.HBM((plane * size, width), jnp.float32),
            bf16(HEAD_SIZE, count),
            bf16(2 * HEAD_SIZE, count),
            pltpu.HBM(out_w.shape, out_w.dtype),
        ],
        "middle_stage",
        3 * 10**9,
        [
            pltpu.VMEM((width, count), jnp.bfloat16),
            pltpu.VMEM((count, width), jnp.bfloat16),
            pltpu.VMEM((count, width), jnp.float32),
            pltpu.SemaphoreType.DMA,
            pltpu.VMEM(out_w.shape, jnp.bfloat16),
            pltpu.SemaphoreType.DMA((FETCHES,)),
        ],
        scalars=1,
        count=6,
        aliases={3: 3},
    )(core, mine, other, out_w, *tri_parts, qkv_w)[:3]


def last_kernel(
    place_ref, mix_ref, out_w, stream_ref, in_w, in_other, down_w, down_other,
    own_ref, part_ref, _same_w, _same_stream, rows, out_rows, sems, sem,
):
    copies = fetch(out_w, out_rows, sems)
    carry = pltpu.make_async_copy(stream_ref, rows, sem)
    carry.start()
    plane, size, width = part_ref.shape
    product = fetched_product(mix_ref[...].T, out_rows, copies)
    carry.wait()
    stream = rows[...] + product
    rows[...] = stream
    own_ref[...] = rows[pl.ds(pl.multiple_of(place_ref[1] * size, size), size), :]
    normed = layer_norm(stream).astype(jnp.bfloat16)
    total = jnp.zeros(stream.shape, jnp.float32)
    for up, down in ((in_w, down_w), (in_other, down_other)):
        hidden = jax.nn.gelu(
            jnp.dot(normed, up[...], preferred_element_type=jnp.float32), approximate=True
        ).astype(jnp.bfloat16)
        total = total + jnp.dot(hidden, down[...], preferred_element_type=jnp.float32)
    for i in range(plane):
        part_ref[i] = total[i * size : (i + 1) * size].astype(jnp.bfloat16)


def last_stage(place, mix, out_w, stream, in_w, in_other, down_w, down_other, size):
    count, width = stream.shape
    return kernel_call(
        last_kernel,
        [
            jax.ShapeDtypeStruct((size, width), jnp.float32),
            bf16(count // size, size, width),
            pltpu.HBM(out_w.shape, out_w.dtype),
            pltpu.HBM(stream.shape, stream.dtype),
        ],
        "last_stage",
        4 * 10**9,
        [
            pltpu.VMEM((count, width), jnp.float32),
            pltpu.VMEM(out_w.shape, jnp.bfloat16),
            pltpu.SemaphoreType.DMA((FETCHES,)),
            pltpu.SemaphoreType.DMA,
        ],
        scalars=1,
        count=7,
        aliases={2: 2, 3: 3},
    )(place, mix, out_w, stream, in_w, in_other, down_w, down_other)[:2]


def exchange(values, axes):
    return lax.all_to_all(values, axes, 0, 0, tiled=True)


def copies_kernel(value_ref, out_ref, sems):
    copies = [
        pltpu.make_async_copy(value_ref, out_ref.at[i], sems.at[i]) for i in range(out_ref.shape[0])
    ]
    for copy in copies:
        copy.start()
    for copy in copies:
        copy.wait()


def copies_of(values, count):
    return kernel_call(
        copies_kernel,
        pltpu.HBM((count,) + values.shape, values.dtype),
        "copies",
        10**7,
        [pltpu.SemaphoreType.DMA((count,))],
        count=1,
    )(values)


def other_core(values):
    return lax.ppermute(values, "c", [(0, 1), (1, 0)])


def swap_near(values):
    return lax.ppermute(values, "xl", [(0, 1), (1, 0)])


def gather_head(copies):
    mine = exchange(copies, PLANE)
    return mine, other_core(mine)


def per_device(
    sizes,
    tri_tokens,
    image_tokens,
    cross_q,
    cross_kv,
    cross_out,
    self_qkv,
    self_out,
    mlp_in,
    mlp_out,
):
    size, width = tri_tokens.shape
    plane = sizes["xh"] * sizes["y"]
    z_axes = ("zh", "zl")
    z_count = sizes["zh"] * sizes["zl"]

    def along(values, shift):
        return lax.ppermute(values, z_axes, [(i, (i + shift) % z_count) for i in range(z_count)])

    core = jnp.stack([lax.axis_index("c"), lax.axis_index(PLANE)]).astype(jnp.int32)
    tri_tokens, core = lax.optimization_barrier((tri_tokens, core))
    mine = exchange(copies_of(tri_tokens, plane), PLANE)
    both = project_kv(image_tokens, jnp.swapaxes(cross_kv, 1, 2).reshape(-1, width))
    mine, both, cross_out, self_out = lax.optimization_barrier((mine, both, cross_out, self_out))
    cross_out_all = lax.all_gather(cross_out, HEAD, axis=0, tiled=True)
    self_out_all = lax.all_gather(self_out, HEAD, axis=0, tiled=True)
    other = other_core(mine)
    near = (prepare(both), both)
    tri_parts = (mine, other)
    own = first_stage(core, mine, other, cross_q.T)

    def behind(value, done):
        return value if done is None else lax.optimization_barrier((value, done))[0]

    arrived = {0: own}
    sums = {None: None}

    def relay(block, shift, done):
        arrived[block - shift] = along(behind(arrived[block], sums[done]), shift)

    def near_part(block, done):
        sums[block] = cross_attention(behind(arrived[block], sums[done]), near, [], jnp.float32)

    relay(0, 1, None)
    near_part(0, None)
    relay(0, -1, 0)
    relay(-1, 1, 0)
    near_part(-1, 0)
    relay(1, -1, -1)
    near_part(1, -1)
    relay(-2, 1, 1)
    near_part(-2, 1)
    relay(2, -1, -2)
    near_part(2, -2)
    relay(-3, 1, 2)
    near_part(-3, 2)
    near_part(3, -3)
    swapped = behind(swap_near(both), sums[3])
    far = (prepare(swapped), swapped)
    passed = {}
    last = sums[3]
    for block in (3, -4, 2, -3, 1, -2, -1, 0):
        if block == -4:
            waiting = behind(arrived[-4], last)
            sums[-4] = cross_attention(waiting, near, [], jnp.float32)
            last = sums[-4]
        query = behind(arrived[block], last)
        extras = [sums[block]]
        if block in passed:
            extras.append(passed[block])
        if block == 0:
            break
        last = cross_attention(query, far, extras, jnp.bfloat16)
        step = 1 if block > 0 else -1
        sent = along(last, step)
        if block == step:
            passed[0, step] = sent
        else:
            passed[block - step] = sent
    home = cross_attention(query, far, extras, jnp.bfloat16)
    home, cross_out_all = lax.optimization_barrier((home, cross_out_all))
    slots = finish([home, passed[0, 1], passed[0, -1]], plane, 1)
    mine, other = gather_head(slots)
    self_weight = jnp.swapaxes(self_qkv, 1, 2).reshape(-1, width)
    stream, own, own_kv = middle_stage(
        core, mine, other, cross_out_all, tri_parts, self_weight
    )

    (held_in, held_down), _ = lax.optimization_barrier(((mlp_in, mlp_out), sums[3]))
    in_other, down_other = other_core(held_in), other_core(held_down)
    blocks, near_query = [along(own_kv, 1), along(own_kv, -1)], swap_near(own)
    blocks, near_query = lax.optimization_barrier((blocks, near_query))
    queries = [own, near_query]
    carried, waiting = None, [own_kv]
    for step in range(3):
        held = blocks
        if carried is not None:
            held, carried = lax.optimization_barrier((blocks, carried))
        blocks = [along(held[0], 1)]
        if step < 2:
            blocks.append(along(held[1], -1))
        carried = self_attention(queries, waiting, carried)
        waiting = held
    here, there = self_attention(queries, waiting + blocks, carried, jnp.bfloat16)
    there, self_out_all = lax.optimization_barrier((there, self_out_all))
    slots = finish([here, swap_near(there)], plane * sizes["c"], sizes["c"])
    mix = exchange(slots, HEAD).reshape(width, plane * size)
    own, part = last_stage(
        core, mix, self_out_all, stream, mlp_in, in_other, mlp_out, down_other, size
    )
    collected = jnp.sum(exchange(part, PLANE).astype(jnp.float32), axis=0)
    return (own + collected).astype(jnp.bfloat16)


def solution(mesh):
    sizes = {"zh": 2, "zl": 4, "xl": 2, "xh": 2, "y": 4, "c": 2}
    names = tuple(sizes)
    fine = Mesh(mesh.devices.reshape(tuple(sizes.values())), names)
    tok = ("zh", "zl", "xl")
    return jax.shard_map(
        functools.partial(per_device, sizes),
        mesh=fine,
        in_specs=(
            P(names, None),
            P(tok, None),
            P(None, HEAD),
            P(None, None, HEAD),
            P(HEAD, None),
            P(None, None, HEAD),
            P(HEAD, None),
            P(None, HEAD),
            P(HEAD, None),
        ),
        out_specs=P(names, None),
        check_vma=False,
    )
```

```python
import functools
import math

import jax
import jax.numpy as jnp
from jax import lax
from jax.experimental import pallas as pl
from jax.experimental.pallas import tpu as pltpu
from jax.sharding import Mesh, PartitionSpec as P

HEAD_SIZE = 64
EXT = 80
VMEM_LIMIT = 24 * 2**20
SCORE = 2.5 / math.sqrt(HEAD_SIZE) * math.log2(math.e)
PLANE = ("xh", "y")
HEAD = ("xh", "y", "c")


def layer_norm(values):
    centered = values - jnp.mean(values, axis=-1, keepdims=True)
    return centered * lax.rsqrt(jnp.mean(centered * centered, axis=-1, keepdims=True) + 1e-05)


def column_norm(values):
    return values * lax.rsqrt(jnp.mean(values * values, axis=0, keepdims=True) + 1e-06)


def kernel_call(body, out_shape, name, flops, scratch=(), scalars=0, count=0, aliases={}):
    scalar = [pl.BlockSpec(memory_space=pltpu.SMEM)] * scalars
    return pl.pallas_call(
        body,
        in_specs=scalar
        + [
            pl.BlockSpec(memory_space=pl.ANY if i + scalars in aliases else pltpu.VMEM)
            for i in range(count)
        ],
        input_output_aliases=aliases,
        out_specs=jax.tree.map(
            lambda shape: pl.BlockSpec(
                memory_space=pltpu.VMEM if isinstance(shape, jax.ShapeDtypeStruct) else pl.ANY
            ),
            out_shape,
        ),
        out_shape=out_shape,
        scratch_shapes=scratch,
        compiler_params=pltpu.CompilerParams(vmem_limit_bytes=VMEM_LIMIT),
        cost_estimate=pl.CostEstimate(flops=flops, transcendentals=0, bytes_accessed=2**20),
        name=name,
    )


def bf16(*shape):
    return jax.ShapeDtypeStruct(shape, jnp.bfloat16)


def ones_rows(count):
    row = lax.broadcasted_iota(jnp.int32, (EXT - HEAD_SIZE, count), 0)
    return jnp.where(row == 0, 1.0, 0.0).astype(jnp.bfloat16)


def times(rows, weight):
    return lax.dot_general(
        rows, weight, (((1,), (1,)), ((), ())), preferred_element_type=jnp.float32
    )


def project_kv_kernel(image_ref, weight_ref, both_ref):
    product = times(image_ref[...], weight_ref[...]).T
    both_ref[:HEAD_SIZE] = column_norm(product[:HEAD_SIZE]).astype(jnp.bfloat16)
    both_ref[HEAD_SIZE:] = product[HEAD_SIZE:].astype(jnp.bfloat16)


def project_kv(image_tokens, weight):
    rows, features = image_tokens.shape
    block = 512
    return pl.pallas_call(
        project_kv_kernel,
        grid=(rows // block,),
        in_specs=[
            pl.BlockSpec((block, features), lambda i: (i, 0)),
            pl.BlockSpec(weight.shape, lambda i: (0, 0)),
        ],
        out_specs=pl.BlockSpec((2 * HEAD_SIZE, block), lambda i: (0, i)),
        out_shape=bf16(2 * HEAD_SIZE, rows),
        compiler_params=pltpu.CompilerParams(vmem_limit_bytes=VMEM_LIMIT),
        cost_estimate=pl.CostEstimate(
            flops=6 * 10**9, transcendentals=0, bytes_accessed=rows * features * 2
        ),
        name="project_kv",
    )(image_tokens, weight)


def prepare_kernel(both_ref, key_ref):
    key_ref[...] = both_ref[:HEAD_SIZE].T


def prepare(both):
    return kernel_call(
        prepare_kernel, bf16(both.shape[1], HEAD_SIZE), "prepare", 10**9, count=1
    )(both)


def attend(queries, keys, both, step, ahead):
    total = jnp.zeros((EXT, queries.shape[1]), jnp.float32)
    ones = ones_rows(step)
    starts = list(range(0, keys.shape[0], step))

    def scores_of(first):
        return jnp.dot(
            keys[first : first + step, :], queries, preferred_element_type=jnp.float32
        )

    pending = [scores_of(first) for first in starts[:ahead]]
    for place, first in enumerate(starts):
        if place + ahead < len(starts):
            pending.append(scores_of(starts[place + ahead]))
        weights = jnp.exp2(pending.pop(0)).astype(jnp.bfloat16)
        values = jnp.concatenate([both[HEAD_SIZE:, first : first + step], ones], axis=0)
        total = total + jnp.dot(values, weights, preferred_element_type=jnp.float32)
    return total


def cross_kernel(step, query_ref, key_ref, both_ref, *refs):
    total = attend(query_ref[...], key_ref, both_ref, step, 3)
    for extra in refs[:-1]:
        total = total + extra[...].astype(jnp.float32)
    refs[-1][...] = total.astype(refs[-1].dtype)


def cross_attention(query, piece, extras, kind):
    width = query.shape[1]
    return kernel_call(
        functools.partial(cross_kernel, 256),
        jax.ShapeDtypeStruct((EXT, width), kind),
        "cross_attention",
        16 * HEAD_SIZE * width * piece[0].shape[0],
        count=3 + len(extras),
    )(query, *piece, *extras)


def self_kernel(query_count, piece_count, carried, *refs):
    queries = jnp.concatenate([ref[...] for ref in refs[:query_count]], axis=1)
    pieces = refs[query_count : query_count + piece_count]
    rest = refs[query_count + piece_count :]
    outs = rest[query_count:] if carried else rest
    width = pieces[0].shape[1]
    total = jnp.zeros((EXT, queries.shape[1]), jnp.float32)
    for piece in pieces:
        total = total + attend(queries, piece[:HEAD_SIZE].T, piece, width // 2, 2)
    for i, out in enumerate(outs):
        part = total[:, i * width : (i + 1) * width]
        if carried:
            part = part + rest[i][...]
        out[...] = part.astype(out.dtype)


def self_attention(queries, pieces, carried=None, kind=jnp.float32):
    width = queries[0].shape[1]
    count = len(queries)
    extra = [] if carried is None else carried
    return kernel_call(
        functools.partial(self_kernel, count, len(pieces), carried is not None),
        [jax.ShapeDtypeStruct((EXT, width), kind)] * count,
        "self_attention",
        16 * HEAD_SIZE * width * count * width * len(pieces),
        count=count + len(pieces) + len(extra),
    )(*queries, *pieces, *extra)


def finish_kernel(slots, *refs):
    out_ref = refs[-1]
    total = functools.reduce(
        lambda x, y: x + y, [ref[...].astype(jnp.float32) for ref in refs[:-1]]
    )
    mix = (total[:HEAD_SIZE] / total[HEAD_SIZE : HEAD_SIZE + 1]).astype(jnp.bfloat16)
    width = out_ref.shape[2]
    for i in range(out_ref.shape[0]):
        first = (i % slots) * width
        out_ref[i] = mix[:, first : first + width]


def finish(partials, copies, slots):
    width = partials[0].shape[-1] // slots
    return kernel_call(
        functools.partial(finish_kernel, slots),
        bf16(copies, HEAD_SIZE, width),
        "finish",
        10**8,
        count=len(partials),
    )(*partials)


def place_heads(target, core, mine, other):
    plane, size, _ = mine.shape
    for i in range(plane):
        first = pl.multiple_of((2 * i + core) * size, size)
        target[pl.ds(first, size), :] = mine[i]
        first = pl.multiple_of((2 * i + 1 - core) * size, size)
        target[pl.ds(first, size), :] = other[i]


def place_rows(target, core, mine, other):
    plane, size, _ = mine.shape
    for i in range(plane):
        first = pl.multiple_of((plane * core + i) * size, size)
        target[pl.ds(first, size), :] = mine[i]
        first = pl.multiple_of((plane * (1 - core) + i) * size, size)
        target[pl.ds(first, size), :] = other[i]


def first_kernel(core_ref, mine_ref, other_ref, weight_ref, query_ref, rows):
    place_rows(rows, core_ref[0], mine_ref, other_ref)
    normed = layer_norm(rows[...].astype(jnp.float32)).astype(jnp.bfloat16)
    product = times(normed, weight_ref[...]).T
    query_ref[...] = (column_norm(product) * SCORE).astype(jnp.bfloat16)


def first_stage(core, mine, other, weight):
    plane, size, width = mine.shape
    rows = 2 * plane * size
    return kernel_call(
        first_kernel,
        bf16(HEAD_SIZE, rows),
        "first_stage",
        10**9,
        [pltpu.VMEM((rows, width), jnp.bfloat16)],
        scalars=1,
        count=3,
    )(core, mine, other, weight)


FETCHES = 4


def fetch(source, target, sems):
    size = source.shape[0] // FETCHES
    copies = []
    for i in range(FETCHES):
        rows = pl.ds(i * size, size)
        copies.append(pltpu.make_async_copy(source.at[rows, :], target.at[rows, :], sems.at[i]))
        copies[-1].start()
    return copies


def fetched_product(left, target, copies):
    size = target.shape[0] // FETCHES
    total = None
    for i, copy in enumerate(copies):
        copy.wait()
        part = jnp.dot(
            left[:, i * size : (i + 1) * size],
            target[i * size : (i + 1) * size, :],
            preferred_element_type=jnp.float32,
        )
        total = part if total is None else total + part
    return total


def middle_kernel(
    core_ref, mine_ref, other_ref, out_w, tri_mine, tri_other, qkv_w,
    stream_ref, query_ref, kv_ref, _same_w, mix, rows, whole, sem, out_rows, sems,
):
    copies = fetch(out_w, out_rows, sems)
    core = core_ref[0]
    place_heads(mix, core, mine_ref, other_ref)
    place_rows(rows, core, tri_mine, tri_other)
    stream = rows[...].astype(jnp.float32) + fetched_product(mix[...].T, out_rows, copies)
    whole[...] = stream
    half = stream_ref.shape[0]
    copy = pltpu.make_async_copy(
        whole.at[pl.ds(pl.multiple_of(core * half, half), half), :], stream_ref, sem
    )
    copy.start()
    normed = layer_norm(stream).astype(jnp.bfloat16)
    product = times(normed, qkv_w[...]).T
    query_ref[...] = (column_norm(product[:HEAD_SIZE]) * SCORE).astype(jnp.bfloat16)
    kv_ref[:HEAD_SIZE] = column_norm(product[HEAD_SIZE : 2 * HEAD_SIZE]).astype(jnp.bfloat16)
    kv_ref[HEAD_SIZE:] = product[2 * HEAD_SIZE :].astype(jnp.bfloat16)
    copy.wait()


def middle_stage(core, mine, other, out_w, tri_parts, qkv_w):
    plane, size, width = tri_parts[0].shape
    count = 2 * plane * size
    return kernel_call(
        middle_kernel,
        [
            pltpu.HBM((plane * size, width), jnp.float32),
            bf16(HEAD_SIZE, count),
            bf16(2 * HEAD_SIZE, count),
            pltpu.HBM(out_w.shape, out_w.dtype),
        ],
        "middle_stage",
        3 * 10**9,
        [
            pltpu.VMEM((width, count), jnp.bfloat16),
            pltpu.VMEM((count, width), jnp.bfloat16),
            pltpu.VMEM((count, width), jnp.float32),
            pltpu.SemaphoreType.DMA,
            pltpu.VMEM(out_w.shape, jnp.bfloat16),
            pltpu.SemaphoreType.DMA((FETCHES,)),
        ],
        scalars=1,
        count=6,
        aliases={3: 3},
    )(core, mine, other, out_w, *tri_parts, qkv_w)[:3]


def last_kernel(
    place_ref, mix_ref, out_w, stream_ref, in_w, in_other, down_w, down_other,
    own_ref, part_ref, _same_w, _same_stream, rows, out_rows, sems, sem,
):
    copies = fetch(out_w, out_rows, sems)
    carry = pltpu.make_async_copy(stream_ref, rows, sem)
    carry.start()
    plane, size, width = part_ref.shape
    product = fetched_product(mix_ref[...].T, out_rows, copies)
    carry.wait()
    stream = rows[...] + product
    rows[...] = stream
    own_ref[...] = rows[pl.ds(pl.multiple_of(place_ref[1] * size, size), size), :]
    normed = layer_norm(stream).astype(jnp.bfloat16)
    total = jnp.zeros(stream.shape, jnp.float32)
    for up, down in ((in_w, down_w), (in_other, down_other)):
        hidden = jax.nn.gelu(
            jnp.dot(normed, up[...], preferred_element_type=jnp.float32), approximate=True
        ).astype(jnp.bfloat16)
        total = total + jnp.dot(hidden, down[...], preferred_element_type=jnp.float32)
    for i in range(plane):
        part_ref[i] = total[i * size : (i + 1) * size].astype(jnp.bfloat16)


def last_stage(place, mix, out_w, stream, in_w, in_other, down_w, down_other, size):
    count, width = stream.shape
    return kernel_call(
        last_kernel,
        [
            jax.ShapeDtypeStruct((size, width), jnp.float32),
            bf16(count // size, size, width),
            pltpu.HBM(out_w.shape, out_w.dtype),
            pltpu.HBM(stream.shape, stream.dtype),
        ],
        "last_stage",
        4 * 10**9,
        [
            pltpu.VMEM((count, width), jnp.float32),
            pltpu.VMEM(out_w.shape, jnp.bfloat16),
            pltpu.SemaphoreType.DMA((FETCHES,)),
            pltpu.SemaphoreType.DMA,
        ],
        scalars=1,
        count=7,
        aliases={2: 2, 3: 3},
    )(place, mix, out_w, stream, in_w, in_other, down_w, down_other)[:2]


def exchange(values, axes):
    return lax.all_to_all(values, axes, 0, 0, tiled=True)


def copies_kernel(value_ref, out_ref, sems):
    copies = [
        pltpu.make_async_copy(value_ref, out_ref.at[i], sems.at[i]) for i in range(out_ref.shape[0])
    ]
    for copy in copies:
        copy.start()
    for copy in copies:
        copy.wait()


def copies_of(values, count):
    return kernel_call(
        copies_kernel,
        pltpu.HBM((count,) + values.shape, values.dtype),
        "copies",
        10**7,
        [pltpu.SemaphoreType.DMA((count,))],
        count=1,
    )(values)


def other_core(values):
    return lax.ppermute(values, "c", [(0, 1), (1, 0)])


def swap_near(values):
    return lax.ppermute(values, "xl", [(0, 1), (1, 0)])


def gather_head(copies):
    mine = exchange(copies, PLANE)
    return mine, other_core(mine)


def per_device(
    sizes,
    tri_tokens,
    image_tokens,
    cross_q,
    cross_kv,
    cross_out,
    self_qkv,
    self_out,
    mlp_in,
    mlp_out,
):
    size, width = tri_tokens.shape
    plane = sizes["xh"] * sizes["y"]
    z_axes = ("zh", "zl")
    z_count = sizes["zh"] * sizes["zl"]

    def along(values, shift):
        return lax.ppermute(values, z_axes, [(i, (i + shift) % z_count) for i in range(z_count)])

    core = jnp.stack([lax.axis_index("c"), lax.axis_index(PLANE)]).astype(jnp.int32)
    tri_tokens, core = lax.optimization_barrier((tri_tokens, core))
    mine = exchange(copies_of(tri_tokens, plane), PLANE)
    both = project_kv(image_tokens, jnp.swapaxes(cross_kv, 1, 2).reshape(-1, width))
    mine, both, cross_out, self_out = lax.optimization_barrier((mine, both, cross_out, self_out))
    cross_out_all = lax.all_gather(cross_out, HEAD, axis=0, tiled=True)
    self_out_all = lax.all_gather(self_out, HEAD, axis=0, tiled=True)
    other = other_core(mine)
    near = (prepare(both), both)
    tri_parts = (mine, other)
    own = first_stage(core, mine, other, cross_q.T)

    def behind(value, done):
        return value if done is None else lax.optimization_barrier((value, done))[0]

    arrived = {0: own}
    sums = {None: None}

    def relay(block, shift, done):
        arrived[block - shift] = along(behind(arrived[block], sums[done]), shift)

    def near_part(block, done):
        sums[block] = cross_attention(behind(arrived[block], sums[done]), near, [], jnp.float32)

    relay(0, 1, None)
    relay(0, -1, None)
    near_part(0, None)
    relay(-1, 1, 0)
    near_part(-1, 0)
    relay(1, -1, -1)
    near_part(1, -1)
    relay(-2, 1, 1)
    near_part(-2, 1)
    relay(2, -1, -2)
    near_part(2, -2)
    relay(-3, 1, 2)
    near_part(-3, 2)
    near_part(3, -3)
    swapped = behind(swap_near(both), sums[3])
    far = (prepare(swapped), swapped)
    passed = {}
    last = sums[3]
    for block in (3, -4, 2, -3, 1, -2, -1, 0):
        if block == -4:
            waiting = behind(arrived[-4], last)
            sums[-4] = cross_attention(waiting, near, [], jnp.float32)
            last = sums[-4]
        query = behind(arrived[block], last)
        extras = [sums[block]]
        if block in passed:
            extras.append(passed[block])
        if block == 0:
            break
        last = cross_attention(query, far, extras, jnp.bfloat16)
        step = 1 if block > 0 else -1
        sent = along(last, step)
        if block == step:
            passed[0, step] = sent
        else:
            passed[block - step] = sent
    home = cross_attention(query, far, extras, jnp.bfloat16)
    home, cross_out_all = lax.optimization_barrier((home, cross_out_all))
    slots = finish([home, passed[0, 1], passed[0, -1]], plane, 1)
    mine, other = gather_head(slots)
    self_weight = jnp.swapaxes(self_qkv, 1, 2).reshape(-1, width)
    stream, own, own_kv = middle_stage(
        core, mine, other, cross_out_all, tri_parts, self_weight
    )

    (held_in, held_down), _ = lax.optimization_barrier(((mlp_in, mlp_out), sums[3]))
    in_other, down_other = other_core(held_in), other_core(held_down)
    blocks, near_query = [along(own_kv, 1), along(own_kv, -1)], swap_near(own)
    blocks, near_query = lax.optimization_barrier((blocks, near_query))
    queries = [own, near_query]
    carried, waiting = None, [own_kv]
    for step in range(3):
        held = blocks
        if carried is not None:
            held, carried = lax.optimization_barrier((blocks, carried))
        blocks = [along(held[0], 1)]
        if step < 2:
            blocks.append(along(held[1], -1))
        carried = self_attention(queries, waiting, carried)
        waiting = held
    here, there = self_attention(queries, waiting + blocks, carried, jnp.bfloat16)
    there, self_out_all = lax.optimization_barrier((there, self_out_all))
    slots = finish([here, swap_near(there)], plane * sizes["c"], sizes["c"])
    mix = exchange(slots, HEAD).reshape(width, plane * size)
    own, part = last_stage(
        core, mix, self_out_all, stream, mlp_in, in_other, mlp_out, down_other, size
    )
    collected = jnp.sum(exchange(part, PLANE).astype(jnp.float32), axis=0)
    return (own + collected).astype(jnp.bfloat16)


def solution(mesh):
    sizes = {"zh": 2, "zl": 4, "xl": 2, "xh": 2, "y": 4, "c": 2}
    names = tuple(sizes)
    fine = Mesh(mesh.devices.reshape(tuple(sizes.values())), names)
    tok = ("zh", "zl", "xl")
    return jax.shard_map(
        functools.partial(per_device, sizes),
        mesh=fine,
        in_specs=(
            P(names, None),
            P(tok, None),
            P(None, HEAD),
            P(None, None, HEAD),
            P(HEAD, None),
            P(None, None, HEAD),
            P(HEAD, None),
            P(None, HEAD),
            P(HEAD, None),
        ),
        out_specs=P(names, None),
        check_vma=False,
    )
```
